256 devices in a mesh: tiles: 128 (over x, z, y), chan: 2 (over core).
Axes of the slice: x: 4, y: 4, z: 8, core: 2. Of those that a mesh axis runs over, the one named last changes fastest.
Arguments:
- features: bfloat16 [64, 16384, 256], P('chan', 'tiles'), may hold values from -6 to 6
- tile_valid: int32 [2048, 32], P('tiles'), may hold values 0 or 1
- parent_owner: int32 [16384], P('tiles'), may hold values from 0 to 127, as said below
- w_first: bfloat16 [9, 64, 64], P(None, 'chan'), may hold values from -0.25 to 0.25
- w_second: bfloat16 [9, 64, 64], P(None, 'chan'), may hold values from -0.25 to 0.25
- w_merge: bfloat16 [4, 64, 64], P(None, None, 'chan'), may hold values from -0.375 to 0.375
Outputs:
- enhanced: bfloat16 [64, 16384, 256], P('chan', 'tiles')
- parents: bfloat16 [64, 24576, 64], P('chan', 'tiles')
The draws below stay inside these ranges and needn't reach their ends.
Inputs may be any that keep to these rules, and one draw needn't show every extreme that they name: `parent_owner`: within the 128 parents whose children lie on one index of tiles, no owner appears more than 2 times, and some owner appears exactly 2 times for some index. Half of the owners own 3 * 64 parents in all, the other half 128 / 2.
All inputs are finite; a program needn't handle non-finite values. No bound on the sum of `tile_valid` on one device may be relied on, other than what follows from the above.
Results may differ from the reference program's by a relative error of at most 0.0052.
Values may be sent and summed in bfloat16 or wider, within the bound.
A program may use at most 128 MiB of HBM per device.

```python
import jax
import jax.numpy as jnp
from jax import lax

C = 64
TS = 8
NB = 32
GD = 16
W = 256
NG = 2048
H = 16384
PD = 128
OWN_CAP = 192
N_TILES = 128


def draw_parent_owner(key, part):
    devices = N_TILES
    half_devices = devices // 2
    key_kind, key_label, key_shuffle = jax.random.split(key, 3)
    kind_order = jax.random.permutation(key_kind, devices).astype(jnp.int32)
    position = jnp.argsort(kind_order, stable=True).astype(jnp.int32)
    spread_kind = position < half_devices
    sub_index = jnp.where(spread_kind, position, position - half_devices)
    row_ids = jnp.arange(PD, dtype=jnp.int32)
    spread_owner = (sub_index[:, None] * PD + row_ids[None, :]) % devices
    heavy_owner = (sub_index[:, None] * (PD // 2) + row_ids[None, :] // 2) % half_devices
    virtual = jnp.where(spread_kind[:, None], spread_owner, heavy_owner)
    labels = jax.random.permutation(key_label, devices).astype(jnp.int32)
    owner_rows = jnp.take(labels, virtual)
    shuffle_keys = jax.random.split(key_shuffle, devices)
    shuffles = jax.vmap(lambda one_key: jax.random.permutation(one_key, PD))(shuffle_keys)
    shuffled = jnp.take_along_axis(owner_rows, shuffles, axis=1)
    return shuffled.reshape(-1).astype(jnp.int32)


def place_ends(result, stream_key, smallest, high):
    longest = result.shape.index(max(result.shape))
    spots = []
    for shift in (0, 1):
        where = [jax.random.randint(jax.random.fold_in(stream_key, axis), (), 0, length) for axis, length in enumerate(result.shape)]
        where[longest] = (where[longest] + shift) % result.shape[longest]
        spots.append(tuple(where))
    return result.at[spots[0]].set(smallest).at[spots[1]].set(high)


def level_of(stream_key, dims, cuts, low, largest):
    factor_of, own = 1.0, jax.random.fold_in(stream_key, 6)
    for axis_at, blocks in cuts:
        steps = jnp.exp(jax.random.uniform(jax.random.fold_in(own, axis_at), (blocks,), jnp.float32, low / len(cuts), largest / len(cuts)))
        factor_of = factor_of * jnp.repeat(steps, dims[axis_at] // blocks).reshape([-1 if axis == axis_at else 1 for axis in range(len(dims))])
    return factor_of


def centred(stream_key, dims, scale, reach, cuts=(), held_as=jnp.bfloat16):
    gain = level_of(stream_key, dims, cuts, -0.22, 0.18) if cuts else 1.0
    drawn = jax.random.normal(stream_key, dims, jnp.float32) * scale * gain
    return jnp.minimum(jnp.maximum(drawn, -reach), reach).astype(held_as)


def setup_inputs(seed: int = 0) -> dict:
    key_list = jax.random.split(jax.random.key(seed), 7)
    return {
        "features": centred(key_list[0], (C, H, W), 1.0, 6.0, ((0, 2), (1, 128))),
        "tile_valid": place_ends((jax.random.randint(key_list[1], (NG, NB), 0, 8) < 7).astype(jnp.int32), jax.random.fold_in(key_list[1], 1), 0, 1),
        "parent_owner": draw_parent_owner(jax.random.fold_in(key_list[6], 71), 0),
        "w_first": centred(key_list[3], (9, C, C), (9 * C) ** -0.5, 0.25, ((1, 2),)),
        "w_second": centred(key_list[4], (9, C, C), (9 * C) ** -0.5, 0.25, ((1, 2),)),
        "w_merge": centred(key_list[5], (4, C, C), (4 * C) ** -0.5, 0.375, ((2, 2),)),
    }


def dilated(source, weights, dilation):
    kernel = weights.reshape(3, 3, weights.shape[1], weights.shape[2]).transpose(2, 3, 0, 1)
    return lax.conv_general_dilated(source[None], kernel, (1, 1), ((0, 0), (dilation, dilation)), rhs_dilation=(dilation, dilation), dimension_numbers=("NCHW", "OIHW", "NCHW"), preferred_element_type=jnp.float32)[0]


def reference(features, tile_valid, parent_owner, w_first, w_second, w_merge):
    channels = features.shape[0]
    row_count = GD * TS
    col_count = NB * TS
    cell_mask = jnp.broadcast_to(tile_valid.astype(jnp.float32)[:, None, :, None], (tile_valid.shape[0], TS, NB, TS)).reshape(-1, col_count)
    padded = jnp.pad(features, ((0, 0), (3, 3), (0, 0)))
    mask_pad = jnp.pad(cell_mask, ((3, 3), (0, 0)))

    def one_block(block_index):
        offset = (block_index * row_count).astype(jnp.int32)
        row_slab = lax.dynamic_slice_in_dim(padded, offset, row_count + 6, 1)
        mask_slab = lax.dynamic_slice_in_dim(mask_pad, offset, row_count + 6, 0)
        first_out = dilated(row_slab, w_first, 1)
        hidden = jnp.maximum(first_out * mask_slab[None, 1:-1], 0.0).astype(jnp.bfloat16)
        second_out = dilated(hidden, w_second, 2)
        enhanced = (mask_slab[None, 3:-3] * (row_slab[:, 3:-3].astype(jnp.float32) + second_out)).astype(jnp.bfloat16)
        taps_view = enhanced.astype(jnp.float32).reshape(channels, row_count // 2, 2, col_count // 2, 2)
        merged = jnp.zeros((channels, row_count // 2, col_count // 2), jnp.float32)
        for row_tap in range(2):
            for col_tap in range(2):
                merged = merged + jnp.einsum("oi,irc->orc", w_merge[2 * row_tap + col_tap].astype(jnp.float32), taps_view[:, :, row_tap, :, col_tap], precision=lax.Precision.HIGHEST)
        return enhanced, merged.astype(jnp.bfloat16)

    enhanced, merged = lax.map(one_block, jnp.arange(N_TILES, dtype=jnp.int32))
    enhanced_whole = enhanced.transpose(1, 0, 2, 3).reshape(channels, N_TILES * row_count, col_count)
    parent_tiles = merged.reshape(N_TILES, channels, GD // 2, TS, NB // 2, TS).transpose(1, 0, 2, 4, 3, 5).reshape(channels, -1, TS * TS)
    parent_count = parent_owner.shape[0]
    sorted_order = jnp.argsort(parent_owner, stable=True).astype(jnp.int32)
    counts = jax.ops.segment_sum(jnp.ones((parent_count,), jnp.int32), parent_owner, num_segments=N_TILES)
    starts = jnp.cumsum(counts) - counts
    sorted_owner = parent_owner[sorted_order]
    rank_sorted = jnp.arange(parent_count, dtype=jnp.int32) - starts[sorted_owner].astype(jnp.int32)
    rank_in_owner = jnp.zeros((parent_count,), jnp.int32).at[sorted_order].set(rank_sorted.astype(jnp.int32))
    slot_index = parent_owner * OWN_CAP + rank_in_owner
    parents = jnp.zeros((channels, N_TILES * OWN_CAP, TS * TS), jnp.bfloat16).at[:, slot_index].set(parent_tiles)
    return enhanced_whole, parents
```

```python
import functools

import jax
import jax.numpy as jnp
from jax import lax
from jax.experimental import pallas as pl
from jax.experimental.pallas import tpu as pltpu
from jax.sharding import PartitionSpec as P

MESH = pl.DeviceIdType.MESH
F32, BF16 = jnp.float32, jnp.bfloat16
NT = 128
ROWS = 128
COLS = 256
HALF = 64
CH = 64
HC = 32
PAR = 128
CAP = 192
EMPTY = 2.0**100


def dot(a, b):
    return jnp.dot(a, b, preferred_element_type=F32)


def shifted_sum(z, shift, col):
    left = jnp.where(col >= shift, pltpu.roll(z[0:128], shift, 1), 0.0)
    right = jnp.where(col < COLS - shift, pltpu.roll(z[256:384], COLS - shift, 1), 0.0)
    return z[128:256] + left + right


def main_kernel(
    feat, mask, owner, w1h, w2h, wmh, perm,
    enh_out, recv,
    x, h, e, w1, w2, wm, mext, t1, tiles, tall, sel, s32, send,
    loc, snd, rcv, esem, tsem, asem,
):
    t = lax.axis_index("tiles")
    c = lax.axis_index("chan")
    sib = 1 - c
    down = lax.rem(t + 1, NT)
    up = lax.rem(t + NT - 1, NT)

    bar = pltpu.get_barrier_semaphore()

    def greet(i, carry):
        pl.semaphore_signal(
            bar, inc=1, device_id={"tiles": lax.rem(t + i, NT), "chan": c}, device_id_type=MESH
        )
        return carry

    lax.fori_loop(1, NT, greet, 0)
    pl.semaphore_signal(bar, inc=1, device_id={"tiles": t, "chan": sib}, device_id_type=MESH)
    pl.semaphore_signal(bar, inc=1, device_id={"tiles": down, "chan": sib}, device_id_type=MESH)
    pl.semaphore_signal(bar, inc=1, device_id={"tiles": up, "chan": sib}, device_id_type=MESH)
    pl.semaphore_wait(bar, NT + 2)

    my_ch = pl.ds(pl.multiple_of(c * HC, HC), HC)
    local = [
        (feat.at[pl.ds(61 * c, 67)], x.at[pl.ds(3 - 3 * c, 67), my_ch]),
        (mask.at[pl.ds(7 * c, 9)], mext.at[pl.ds(1 - c, 9)]),
        (w1h, w1.at[:, my_ch]),
        (w2h, w2.at[:, my_ch]),
        (wmh, wm.at[:, my_ch]),
    ]
    local = [pltpu.make_async_copy(a, b, loc.at[i]) for i, (a, b) in enumerate(local)]

    def remote(src, dst, ssem, rsem, tile, core):
        return pltpu.make_async_remote_copy(
            src, dst, ssem, rsem, device_id={"tiles": tile, "chan": core}, device_id_type=MESH
        )

    far = [
        remote(w1h, w1.at[:, my_ch], snd.at[0], rcv.at[0], t, sib),
        remote(feat.at[pl.ds(61 * sib, 67)], x.at[pl.ds(3 * c, 67), my_ch], snd.at[1], rcv.at[1], t, sib),
        remote(w2h, w2.at[:, my_ch], snd.at[2], rcv.at[2], t, sib),
        remote(wmh, wm.at[:, my_ch], snd.at[3], rcv.at[3], t, sib),
        remote(
            mask.at[pl.ds(15 - 15 * c, 1)], mext.at[pl.ds(9 * c, 1)], snd.at[4], rcv.at[4],
            lax.rem(t + 1 - 2 * c + NT, NT), c,
        ),
    ]
    halo = [
        remote(feat.at[pl.ds(ROWS - 3, 3)], x.at[pl.ds(0, 3), my_ch], snd.at[5], rcv.at[5 + c], down, 0),
        remote(feat.at[pl.ds(0, 3)], x.at[pl.ds(67, 3), my_ch], snd.at[6], rcv.at[5 + c], up, 1),
    ]
    for copy in halo + far + local:
        copy.start()

    own_row = jnp.broadcast_to(owner[...], (PAR, PAR))
    own_col = jnp.transpose(own_row.astype(F32))
    row_id = lax.broadcasted_iota(jnp.int32, (PAR, PAR), 0)
    col_id = lax.broadcasted_iota(jnp.int32, (PAR, PAR), 1)
    before = jnp.where((own_col == own_row.astype(F32)) & (row_id < col_id), 1.0, 0.0)
    rank = jnp.sum(before, axis=0, keepdims=True)
    for k in range(2):
        hit = (row_id == own_row) & (jnp.broadcast_to(rank, (PAR, PAR)) == float(k))
        sel[pl.ds(k * PAR, PAR)] = jnp.where(hit, 1.0, 0.0).astype(BF16)

    for copy in far + halo:
        copy.wait_send()
    for copy in local:
        copy.wait()
    for copy in far:
        copy.wait_recv()
    edge = x.at[pl.ds(67 * c, 3), pl.ds(0, HC)]
    for k in range(2):
        pltpu.make_async_copy(edge, edge, rcv.at[5 + k]).wait()

    @pl.when((t == 0) & (c == 0))
    def _():
        x[pl.ds(0, 3)] = jnp.zeros((3, CH, COLS), BF16)
        mext[pl.ds(0, 1)] = jnp.zeros((1, 8, COLS), F32)

    @pl.when((t == NT - 1) & (c == 1))
    def _():
        x[pl.ds(67, 3)] = jnp.zeros((3, CH, COLS), BF16)
        mext[pl.ds(9, 1)] = jnp.zeros((1, 8, COLS), F32)

    col = lax.broadcasted_iota(jnp.int32, (128, COLS), 1)

    def conv_one(m, carry):
        z = dot(w1[...].reshape(384, 256), x[pl.ds(2 * m, 4)].reshape(256, COLS))
        out = shifted_sum(z, 1, col).reshape(16, 8, COLS) * mext[(m + 3) // 4][None]
        out = jnp.maximum(out, 0.0).reshape(2, CH, COLS).astype(BF16)
        h[0, m] = out[0]
        h[1, m] = out[1]
        return carry

    lax.fori_loop(0, 34, conv_one, 0)

    def conv_two(q, carry):
        for n2 in range(2):
            n = 2 * q + n2
            for p in range(2):
                z = dot(w2[...].reshape(384, 256), h[p, pl.ds(2 * n, 4)].reshape(256, COLS))
                out = shifted_sum(z, 2, col).reshape(2, CH, COLS)
                for i in range(2):
                    r = 4 * n + p + 2 * i
                    row = (out[i] + x[r + 3].astype(F32)).reshape(8, 8, COLS)
                    row = row * mext[1 + q][None]
                    e[r] = row.reshape(CH, COLS).astype(BF16)
            four = e[pl.ds(4 * n, 4)].reshape(256, COLS)
            turned = lax.dot_general(
                perm[...], four, (((1,), (1,)), ((), ())), preferred_element_type=F32
            ).astype(BF16)
            t1[q, :, pl.ds(n2 * 256, 256)] = turned[0:128]
            t1[q, :, pl.ds(512 + n2 * 256, 256)] = turned[128:256]
        return carry

    lax.fori_loop(0, 8, conv_two, 0)

    e_own = pltpu.make_async_copy(e.at[:, my_ch], enh_out.at[pl.ds(HALF * c, HALF)], loc.at[0])
    e_own.start()
    e_far = remote(
        e.at[:, pl.ds(pl.multiple_of(sib * HC, HC), HC)], enh_out.at[pl.ds(HALF * c, HALF)],
        esem.at[0], esem.at[1], t, sib,
    )
    e_far.start()

    for q in range(8):
        g, tp = q // 2, q % 2
        merged = dot(t1[q], wm[...].reshape(1024, 256)).astype(BF16)
        for v in range(8):
            for k in range(2):
                tiles[k, pl.ds(g * 16, 16), pl.ds((v * 2 + tp) * 128, 128)] = merged[
                    v * 16 : v * 16 + 16, k * 128 : k * 128 + 128
                ]

    mine = pl.ds(pl.multiple_of(c * HALF, HALF), HALF)
    t_own = pltpu.make_async_copy(tiles.at[c], tall.at[mine], loc.at[1])
    t_far = remote(tiles.at[sib], tall.at[mine], tsem.at[0], tsem.at[1], t, sib)
    t_far.start()
    t_own.start()
    t_own.wait()
    t_far.wait()

    filled = jnp.sum(sel[...].astype(F32), axis=1, keepdims=True)
    for v in range(8):
        out = dot(sel[...], tall[:, pl.ds(v * 256, 256)])
        if v == 0:
            out = jnp.where(jnp.broadcast_to(filled, (256, 256)) > 0.5, out, EMPTY)
        for k in range(2):
            for d2 in range(2):
                s32[d2, pl.ds(v * 2 + k, 128, stride=16), :] = out[
                    k * 128 : k * 128 + 128, d2 * 128 : d2 * 128 + 128
                ]

    def narrow(i, carry):
        for d2 in range(2):
            part = s32[d2, pl.ds(pl.multiple_of(128 * i, 128), 128)]
            send[pl.ds(8 * i, 8), :, pl.ds(d2 * 128, 128)] = part.astype(BF16).reshape(8, 16, 128)
        return carry

    lax.fori_loop(0, 16, narrow, 0)

    def deliver(i, carry):
        d = lax.rem(t + i, NT)
        remote(send.at[d], recv.at[t], asem.at[0], asem.at[1], d, c).start()
        return carry

    lax.fori_loop(1, NT, deliver, 0)
    own = pltpu.make_async_copy(send.at[t], recv.at[t], loc.at[2])
    own.start()
    own.wait()
    e_own.wait()
    e_far.wait()
    others = recv.at[pl.ds(0, NT - 1)]
    gone = send.at[pl.ds(0, NT - 1)]
    pltpu.make_async_copy(gone, gone, asem.at[0]).wait()
    pltpu.make_async_copy(others, others, asem.at[1]).wait()


def main_call(feat, mask, owner, w1h, w2h, wmh, perm):
    any_ = pl.BlockSpec(memory_space=pl.ANY)
    vmem = pl.BlockSpec(memory_space=pltpu.VMEM)
    return pl.pallas_call(
        main_kernel,
        out_shape=(
            jax.ShapeDtypeStruct((ROWS, HC, COLS), BF16),
            jax.ShapeDtypeStruct((NT, 16, 256), BF16),
        ),
        in_specs=[any_, any_, vmem, any_, any_, any_, vmem],
        out_specs=(any_, any_),
        scratch_shapes=[
            pltpu.VMEM((70, CH, COLS), BF16),
            pltpu.VMEM((2, 34, CH, COLS), BF16),
            pltpu.VMEM((HALF, CH, COLS), BF16),
            pltpu.VMEM((6, CH, 256), BF16),
            pltpu.VMEM((6, CH, 256), BF16),
            pltpu.VMEM((16, CH, 256), BF16),
            pltpu.VMEM((10, 8, COLS), F32),
            pltpu.VMEM((8, 128, 1024), BF16),
            pltpu.VMEM((2, HALF, 2048), BF16),
            pltpu.VMEM((PAR, 2048), BF16),
            pltpu.VMEM((256, PAR), BF16),
            pltpu.VMEM((2, 2048, 128), F32),
            pltpu.VMEM((NT, 16, 256), BF16),
            pltpu.SemaphoreType.DMA((5,)),
            pltpu.SemaphoreType.DMA((7,)),
            pltpu.SemaphoreType.DMA((7,)),
            pltpu.SemaphoreType.DMA((2,)),
            pltpu.SemaphoreType.DMA((2,)),
            pltpu.SemaphoreType.DMA((2,)),
        ],
        compiler_params=pltpu.CompilerParams(
            collective_id=0, has_side_effects=True, vmem_limit_bytes=40 << 20
        ),
        name="convs_and_exchange",
    )(feat, mask, owner, w1h, w2h, wmh, perm)


def place_kernel(recv, p1, p2, out, r32, o):
    def widen(i, carry):
        for d2 in range(2):
            part = recv[pl.ds(8 * i, 8), :, pl.ds(d2 * 128, 128)].reshape(128, 128)
            r32[d2, pl.ds(pl.multiple_of(128 * i, 128), 128)] = part.astype(F32)
        return carry

    lax.fori_loop(0, 16, widen, 0)
    here = [jnp.where(r32[0, pl.ds(k, 128, stride=16), :] < EMPTY, 1.0, 0.0) for k in range(2)]
    first = (lax.broadcasted_iota(jnp.int32, (8, NT), 1) == 0).astype(BF16)
    count = lax.dot_general(
        first, (here[0] + here[1]).astype(BF16), (((1,), (1,)), ((), ())),
        preferred_element_type=F32,
    )
    src = lax.broadcasted_iota(jnp.int32, (NT, NT), 0)
    dst = lax.broadcasted_iota(jnp.int32, (NT, NT), 1)
    start = dot(count.astype(BF16), jnp.where(src < dst, 1.0, 0.0).astype(BF16))
    slot = lax.broadcasted_iota(jnp.int32, (CAP, NT), 0).astype(F32)
    count = jnp.broadcast_to(count[0:1], (CAP, NT))
    start = jnp.broadcast_to(start[0:1], (CAP, NT))
    pick = jnp.concatenate(
        [
            jnp.where((slot == start + float(k)) & (count > float(k)), 1.0, 0.0)
            for k in range(2)
        ],
        axis=1,
    ).astype(BF16)

    for v in range(8):
        got = jnp.concatenate(
            [
                jnp.concatenate(
                    [r32[d2, pl.ds(v * 2 + k, 128, stride=16), :] for d2 in range(2)], axis=1
                )
                for k in range(2)
            ],
            axis=0,
        ).astype(BF16)
        placed = dot(pick, got).astype(BF16)
        o[v] = dot(placed, p1[...])
    lane = lax.broadcasted_iota(jnp.int32, (CAP, 128), 1) // 32
    for q in range(8):
        w, pos = q // 4, q % 4
        halves = []
        for hv in range(2):
            acc = jnp.zeros((CAP, 128), F32)
            for i in range(4):
                part = o[hv * 4 + i, :, pl.ds(w * 128, 128)]
                if i != pos:
                    part = pltpu.roll(part, (32 * (i - pos)) % 128, 1)
                acc = jnp.where(lane == i, part, acc)
            halves.append(acc)
        last = dot(jnp.concatenate(halves, axis=1).astype(BF16), p2[...]).astype(BF16)
        for i in range(4):
            out[q * 4 + i] = last[:, i * 64 : i * 64 + 64]


def place_call(recv, p1, p2):
    vmem = pl.BlockSpec(memory_space=pltpu.VMEM)
    return pl.pallas_call(
        place_kernel,
        out_shape=jax.ShapeDtypeStruct((HC, CAP, 64), BF16),
        in_specs=[vmem, vmem, vmem],
        out_specs=vmem,
        scratch_shapes=[pltpu.VMEM((2, 2048, 128), F32), pltpu.VMEM((8, CAP, 256), F32)],
        compiler_params=pltpu.CompilerParams(vmem_limit_bytes=40 << 20),
        name="place_parents",
    )(recv, p1, p2)


def one_hot(index, size):
    return (index[:, None] == jnp.arange(size, dtype=jnp.int32)[None, :]).astype(BF16)


def toeplitz(w):
    taps = w.reshape(3, 3, HC, CH).transpose(1, 2, 0, 3).reshape(3, HC, 3 * CH)
    return jnp.stack(
        [
            jnp.pad(taps, ((0, 0), (0, 0), (0, CH))),
            jnp.pad(taps, ((0, 0), (0, 0), (CH, 0))),
        ],
        axis=1,
    ).reshape(6, HC, 4 * CH)


def merge_weights(w):
    w = w.reshape(2, 2, 2, HC, HC).transpose(1, 0, 4, 2, 3)
    eye = jnp.eye(4, dtype=BF16)
    full = w[:, None, :, :, :, None, :] * eye[None, :, None, None, None, :, None]
    return full.reshape(16, HC, 256)


def on_device(features, tile_valid, parent_owner, w_first, w_second, w_merge):
    feat = jnp.transpose(features, (1, 0, 2))
    mask = jnp.broadcast_to(
        jnp.repeat(tile_valid.astype(F32), 8, axis=1)[:, None, :], (16, 8, COLS)
    )
    ids = jnp.arange(256, dtype=jnp.int32)
    b, v, j = ids // 128, ids // 16 % 8, ids % 16
    perm = one_hot(16 * j + 2 * v + b, 256)
    u, o = ids // 32, ids % 32
    p1 = one_hot(o // 4 * 32 + u * 4 + o % 4, 256)
    v2, u2, o2 = ids // 32, ids // 4 % 8, ids % 4
    p2 = one_hot(o2 * 64 + u2 * 8 + v2, 256)
    enh, recv = main_call(
        feat, mask, parent_owner.reshape(1, PAR), toeplitz(w_first), toeplitz(w_second),
        merge_weights(w_merge), perm,
    )
    parents = place_call(recv, p1, p2)
    return (jnp.transpose(enh, (1, 0, 2)), parents)


def solution(mesh):
    return jax.shard_map(
        on_device,
        mesh=mesh,
        in_specs=(
            P("chan", "tiles", None),
            P("tiles", None),
            P("tiles"),
            P(None, "chan", None),
            P(None, "chan", None),
            P(None, None, "chan"),
        ),
        out_specs=(P("chan", "tiles", None), P("chan", "tiles", None)),
        check_vma=False,
    )
```

```python
import functools

import jax
import jax.numpy as jnp
from jax import lax
from jax.experimental import pallas as pl
from jax.experimental.pallas import tpu as pltpu
from jax.sharding import PartitionSpec as P

MESH = pl.DeviceIdType.MESH
F32, BF16 = jnp.float32, jnp.bfloat16
NT = 128
ROUNDS = 7
ROWS = 128
COLS = 256
HALF = 64
CH = 64
HC = 32
PAR = 128
CAP = 192
EMPTY = 2.0**100


def dot(a, b):
    return jnp.dot(a, b, preferred_element_type=F32)


def dot_t(a, b):
    return lax.dot_general(a, b, (((1,), (1,)), ((), ())), preferred_element_type=F32)


def ones_at(shape, test):
    row = lax.broadcasted_iota(jnp.int32, shape, 0)
    col = lax.broadcasted_iota(jnp.int32, shape, 1)
    return jnp.where(test(row, col), 1.0, 0.0).astype(BF16)


def shifted_sum(z, shift, col):
    left = jnp.where(col >= shift, pltpu.roll(z[0:128], shift, 1), 0.0)
    right = jnp.where(col < COLS - shift, pltpu.roll(z[256:384], COLS - shift, 1), 0.0)
    return z[128:256] + left + right


def main_kernel(
    feat, valid, owner, w1raw, w2raw, wmraw,
    enh_out, recv,
    fv, f32t, x, h, e32, et, w1r, w2r, wmr, w1, w2, wm, near, mall, t1, tiles, tall, sel, s32, send,
    fsem, wsem, wsend, wrecv, xsend, xrecv, hsend, hrecv, bsem, esem, tsem, asem,
):
    t = lax.axis_index("tiles")
    c = lax.axis_index("chan")
    sib = 1 - c
    down = lax.rem(t + 1, NT)
    up = lax.rem(t + NT - 1, NT)
    base = HALF * c

    def remote(src, dst, ssem, rsem, tile, core):
        return pltpu.make_async_remote_copy(
            src, dst, ssem, rsem, device_id={"tiles": tile, "chan": core}, device_id_type=MESH
        )

    def partner(r):
        bit = lax.rem(t // 2**r, 2)
        return t + 2**r - bit * 2 ** (r + 1)

    bar = pltpu.get_barrier_semaphore()
    near_by = [(t, sib), (down, 0), (down, 1), (up, 0), (up, 1)]
    for tile, core in near_by + [(partner(r), c) for r in range(ROUNDS)]:
        pl.semaphore_signal(
            bar, inc=1, device_id={"tiles": tile, "chan": core}, device_id_type=MESH
        )

    def chunk_of(i, core):
        return lax.rem(i + 3 * (1 - core), 8)

    def load(i):
        rows = pl.ds(pl.multiple_of(16 * chunk_of(i, c), 16), 16)
        return pltpu.make_async_copy(feat.at[:, rows], fv.at[:, rows], fsem.at[i])

    for i in range(8):
        load(i).start()
    my_ch = pl.ds(pl.multiple_of(c * HC, HC), HC)
    pieces = [(w1raw, w1r.at[:, my_ch]), (w2raw, w2r.at[:, my_ch]), (wmraw, wmr.at[:, my_ch])]
    w_own = [pltpu.make_async_copy(a, b, wsem.at[i]) for i, (a, b) in enumerate(pieces)]
    w_far = [remote(a, b, wsend.at[i], wrecv.at[i], t, sib) for i, (a, b) in enumerate(pieces)]
    w_far.append(remote(valid, near, wsend.at[3], wrecv.at[3], lax.rem(t + 1 - 2 * c + NT, NT), c))
    for copy in w_own:
        copy.start()

    own_row = jnp.broadcast_to(owner[...], (PAR, PAR))
    own_col = jnp.transpose(own_row.astype(F32))
    row_id = lax.broadcasted_iota(jnp.int32, (PAR, PAR), 0)
    col_id = lax.broadcasted_iota(jnp.int32, (PAR, PAR), 1)
    before = jnp.where((own_col == own_row.astype(F32)) & (row_id < col_id), 1.0, 0.0)
    rank = jnp.sum(before, axis=0, keepdims=True)
    for k in range(2):
        hit = (row_id == own_row) & (jnp.broadcast_to(rank, (PAR, PAR)) == float(k))
        sel[pl.ds(k * PAR, PAR)] = jnp.where(hit, 1.0, 0.0).astype(BF16)

    def turn(i):
        load(i).wait()
        k = chunk_of(i, c)
        rows = pl.ds(pl.multiple_of(16 * k, 16), 16)
        for d2 in range(2):
            f32t[d2] = fv[:, rows, pl.ds(d2 * 128, 128)].astype(F32).reshape(512, 128)
        for r in range(16):
            for d2 in range(2):
                x[3 + 16 * k + r, my_ch, pl.ds(d2 * 128, 128)] = f32t[
                    d2, pl.ds(r, HC, stride=16), :
                ].astype(BF16)

    def x_copy(i, core):
        rows = pl.ds(3 + 16 * chunk_of(i, core), 16)
        part = x.at[rows, pl.ds(pl.multiple_of(core * HC, HC), HC)]
        return remote(part, part, xsend.at[i], xrecv.at[i], t, sib)

    turn(0)
    pl.semaphore_wait(bar, 5 + ROUNDS)

    def signal_round(r):
        pl.semaphore_signal(
            bsem.at[r], inc=1, device_id={"tiles": partner(r), "chan": c}, device_id_type=MESH
        )

    signal_round(0)
    for copy in w_far:
        copy.start()
    x_copy(0, c).start()
    for i in range(1, 8):
        turn(i)
        if i < 5:
            x_copy(i, c).start()
    halo = [
        remote(x.at[pl.ds(ROWS, 3), my_ch], x.at[pl.ds(0, 3), my_ch], hsend.at[0], hrecv.at[c], down, 0),
        remote(x.at[pl.ds(3, 3), my_ch], x.at[pl.ds(131, 3), my_ch], hsend.at[1], hrecv.at[c], up, 1),
    ]
    for copy in halo:
        copy.start()

    for copy in w_own:
        copy.wait()
    for copy in w_far:
        copy.wait_recv()
    for raw, out in ((w1r, w1), (w2r, w2)):
        for first in range(2):
            rows = []
            for b in range(3):
                total = jnp.zeros((CH, 256), F32)
                for a in range(3):
                    place = ones_at((CH, 256), lambda i, j, s=a + first: j == i + CH * s)
                    total = total + dot(raw[3 * a + b], place)
                out[2 * b + first] = total.astype(BF16)
    for tr in range(4):
        place = ones_at((CH, 256), lambda i, j, tr=tr: j == (i // HC) * 128 + tr * HC + i % HC)
        for a in range(2):
            for b in range(2):
                wm[b * 8 + tr * 2 + a] = dot(wmr[2 * a + b], place).astype(BF16)
    spread = ones_at((32, COLS), lambda i, j: i == j // 8)
    mine = dot(valid[...].astype(F32).astype(BF16), spread)
    other = dot(near[...].astype(F32).astype(BF16), spread)
    inside_up = jnp.where(t > 0, 1.0, 0.0).astype(F32)
    inside_down = jnp.where(t < NT - 1, 1.0, 0.0).astype(F32)
    mall[0] = jnp.broadcast_to(other[15:16], (8, COLS)) * inside_up
    mall[17] = jnp.broadcast_to(other[0:1], (8, COLS)) * inside_down
    for i in range(16):
        mall[i + 1] = jnp.broadcast_to(mine[i : i + 1], (8, COLS))

    col = lax.broadcasted_iota(jnp.int32, (128, COLS), 1)

    def conv_one(j):
        m = lax.rem(j + 2 * (1 - c), 34)
        z = dot(w1[...].reshape(384, 256), x[pl.ds(base + 2 * m, 4)].reshape(256, COLS))
        out = shifted_sum(z, 1, col).reshape(16, 8, COLS) * mall[8 * c + (m + 3) // 4][None]
        out = jnp.maximum(out, 0.0).reshape(2, CH, COLS).astype(BF16)
        h[0, m] = out[0]
        h[1, m] = out[1]

    def next_round(r):
        pl.semaphore_wait(bsem.at[r], 1)
        if r + 1 < ROUNDS:
            signal_round(r + 1)

    for phase in range(4):
        for i in (0, 1) if phase == 0 else (phase + 1,):
            x_copy(i, sib).wait_recv()
        if phase:
            next_round(phase - 1)

        def four(k, carry, phase=phase):
            for u in range(4):
                conv_one(8 * phase + 4 * k + u)
            return carry

        lax.fori_loop(0, 2, four, 0)

    edge = x.at[pl.ds(131 * c, 3), pl.ds(0, HC)]
    for k in range(2):
        pltpu.make_async_copy(edge, edge, hrecv.at[k]).wait()

    @pl.when((t == 0) & (c == 0))
    def _():
        x[pl.ds(0, 3)] = jnp.zeros((3, CH, COLS), BF16)

    @pl.when((t == NT - 1) & (c == 1))
    def _():
        x[pl.ds(131, 3)] = jnp.zeros((3, CH, COLS), BF16)

    next_round(3)
    conv_one(32)
    conv_one(33)
    next_round(4)

    perm = ones_at((256, 256), lambda i, j: j == 16 * (i % 16) + 2 * (i // 16 % 8) + i // 128)

    def conv_two(q, carry):
        for n2 in range(2):
            n = 2 * q + n2
            rows = [None] * 4
            for p in range(2):
                z = dot(w2[...].reshape(384, 256), h[p, pl.ds(2 * n, 4)].reshape(256, COLS))
                out = shifted_sum(z, 2, col).reshape(2, CH, COLS)
                for i in range(2):
                    r = 4 * n + p + 2 * i
                    row = (out[i] + x[base + r + 3].astype(F32)).reshape(8, 8, COLS)
                    row = (row * mall[1 + 8 * c + q][None]).reshape(CH, COLS)
                    for d2 in range(2):
                        e32[d2, pl.ds(pl.multiple_of(r * CH, CH), CH)] = row[
                            :, d2 * 128 : d2 * 128 + 128
                        ]
                    rows[p + 2 * i] = row.astype(BF16)
            turned = dot_t(perm, jnp.concatenate(rows, axis=0)).astype(BF16)
            t1[q, :, pl.ds(n2 * 256, 256)] = turned[0:128]
            t1[q, :, pl.ds(512 + n2 * 256, 256)] = turned[128:256]
        return carry

    lax.fori_loop(0, 4, conv_two, 0)
    next_round(5)
    lax.fori_loop(4, 8, conv_two, 0)

    for q in range(8):
        g, tp = q // 2, q % 2
        merged = dot(t1[q], wm[...].reshape(1024, 256)).astype(BF16)
        for v in range(8):
            for k in range(2):
                tiles[k, pl.ds(g * 16, 16), pl.ds((v * 2 + tp) * 128, 128)] = merged[
                    v * 16 : v * 16 + 16, k * 128 : k * 128 + 128
                ]

    my_par = pl.ds(pl.multiple_of(base, HALF), HALF)
    t_own = pltpu.make_async_copy(tiles.at[c], tall.at[my_par], wsem.at[0])
    t_far = remote(tiles.at[sib], tall.at[my_par], tsem.at[0], tsem.at[1], t, sib)
    t_far.start()
    t_own.start()
    filled = jnp.sum(sel[...].astype(F32), axis=1, keepdims=True)
    next_round(6)
    t_own.wait()
    t_far.wait()

    for v in range(8):
        out = dot(sel[...], tall[:, pl.ds(v * 256, 256)])
        if v == 0:
            out = jnp.where(jnp.broadcast_to(filled, (256, 256)) > 0.5, out, EMPTY)
        for k in range(2):
            for d2 in range(2):
                s32[d2, pl.ds(v * 2 + k, 128, stride=16), :] = out[
                    k * 128 : k * 128 + 128, d2 * 128 : d2 * 128 + 128
                ]

    def narrow(i, carry):
        for d2 in range(2):
            part = s32[d2, pl.ds(pl.multiple_of(128 * i, 128), 128)]
            send[pl.ds(8 * i, 8), :, pl.ds(d2 * 128, 128)] = part.astype(BF16).reshape(8, 16, 128)
        return carry

    lax.fori_loop(0, 16, narrow, 0)

    def deliver(i, carry):
        d = lax.rem(t + i, NT)
        remote(send.at[d], recv.at[t], asem.at[0], asem.at[1], d, c).start()
        return carry

    lax.fori_loop(1, NT, deliver, 0)
    own = pltpu.make_async_copy(send.at[t], recv.at[t], wsem.at[1])
    own.start()

    def back(k, carry):
        for d2 in range(2):
            et[k, :, pl.ds(d2 * 128, 128)] = e32[d2, pl.ds(k, HALF, stride=CH), :].astype(BF16)
        return carry

    lax.fori_loop(0, CH, back, 0)
    my_rows = pl.ds(pl.multiple_of(base, HALF), HALF)
    e_own = pltpu.make_async_copy(et.at[my_ch], enh_out.at[:, my_rows], wsem.at[2])
    e_far = remote(
        et.at[pl.ds(pl.multiple_of(sib * HC, HC), HC)], enh_out.at[:, my_rows],
        esem.at[0], esem.at[1], t, sib,
    )
    e_far.start()
    e_own.start()
    for copy in w_far + halo:
        copy.wait_send()
    for i in range(5):
        x_copy(i, c).wait_send()
    own.wait()
    e_own.wait()
    e_far.wait()
    others = recv.at[pl.ds(0, NT - 1)]
    gone = send.at[pl.ds(0, NT - 1)]
    pltpu.make_async_copy(gone, gone, asem.at[0]).wait()
    pltpu.make_async_copy(others, others, asem.at[1]).wait()


def main_call(feat, valid, owner, w1raw, w2raw, wmraw):
    any_ = pl.BlockSpec(memory_space=pl.ANY)
    vmem = pl.BlockSpec(memory_space=pltpu.VMEM)
    dma = pltpu.SemaphoreType.DMA
    return pl.pallas_call(
        main_kernel,
        out_shape=(
            jax.ShapeDtypeStruct((HC, ROWS, COLS), BF16),
            jax.ShapeDtypeStruct((NT, 16, 256), BF16),
        ),
        in_specs=[any_, vmem, vmem, any_, any_, any_],
        out_specs=(any_, any_),
        scratch_shapes=[
            pltpu.VMEM((HC, ROWS, COLS), BF16),
            pltpu.VMEM((2, 512, 128), F32),
            pltpu.VMEM((134, CH, COLS), BF16),
            pltpu.VMEM((2, 34, CH, COLS), BF16),
            pltpu.VMEM((2, HALF * CH, 128), F32),
            pltpu.VMEM((CH, HALF, COLS), BF16),
            pltpu.VMEM((9, CH, CH), BF16),
            pltpu.VMEM((9, CH, CH), BF16),
            pltpu.VMEM((4, CH, CH), BF16),
            pltpu.VMEM((6, CH, 256), BF16),
            pltpu.VMEM((6, CH, 256), BF16),
            pltpu.VMEM((16, CH, 256), BF16),
            pltpu.VMEM((16, 32), jnp.int32),
            pltpu.VMEM((18, 8, COLS), F32),
            pltpu.VMEM((8, 128, 1024), BF16),
            pltpu.VMEM((2, HALF, 2048), BF16),
            pltpu.VMEM((PAR, 2048), BF16),
            pltpu.VMEM((256, PAR), BF16),
            pltpu.VMEM((2, 2048, 128), F32),
            pltpu.VMEM((NT, 16, 256), BF16),
            dma((8,)),
            dma((3,)),
            dma((4,)),
            dma((4,)),
            dma((5,)),
            dma((5,)),
            dma((2,)),
            dma((2,)),
            pltpu.SemaphoreType.REGULAR((ROUNDS,)),
            dma((2,)),
            dma((2,)),
            dma((2,)),
        ],
        compiler_params=pltpu.CompilerParams(
            collective_id=0, has_side_effects=True, vmem_limit_bytes=44 << 20
        ),
        name="convs_and_exchange",
    )(feat, valid, owner, w1raw, w2raw, wmraw)


def place_kernel(recv, enh, out, enh_out, r32, o32, sem):
    move = pltpu.make_async_copy(enh, enh_out, sem)
    move.start()

    def widen(i, carry):
        for d2 in range(2):
            part = recv[pl.ds(8 * i, 8), :, pl.ds(d2 * 128, 128)].reshape(128, 128)
            r32[d2, pl.ds(pl.multiple_of(128 * i, 128), 128)] = part.astype(F32)
        return carry

    lax.fori_loop(0, 16, widen, 0)
    here = [jnp.where(r32[0, pl.ds(k, 128, stride=16), :] < EMPTY, 1.0, 0.0) for k in range(2)]
    count = dot_t(ones_at((8, NT), lambda i, j: j == 0), (here[0] + here[1]).astype(BF16))
    start = dot(count.astype(BF16), ones_at((NT, NT), lambda i, j: i < j))
    slot = lax.broadcasted_iota(jnp.int32, (CAP, NT), 0).astype(F32)
    count = jnp.broadcast_to(count[0:1], (CAP, NT))
    start = jnp.broadcast_to(start[0:1], (CAP, NT))
    pick = jnp.concatenate(
        [
            jnp.where((slot == start + float(k)) & (count > float(k)), 1.0, 0.0)
            for k in range(2)
        ],
        axis=1,
    ).astype(BF16)
    same = ones_at((256, 256), lambda i, j: i == j)
    for v in range(8):
        got = jnp.concatenate(
            [
                jnp.concatenate(
                    [r32[d2, pl.ds(v * 2 + k, 128, stride=16), :] for d2 in range(2)], axis=1
                )
                for k in range(2)
            ],
            axis=0,
        ).astype(BF16)
        turned = dot_t(same, dot(pick, got).astype(BF16))
        for u in range(8):
            part = turned[u * HC : u * HC + HC]
            o32[0, pl.ds(u * 8 + v, HC, stride=64), :] = part[:, 0:128]
            o32[1, pl.ds(u * 8 + v, HC, stride=64), pl.ds(0, 64)] = part[:, 128:CAP]

    def narrow(k, carry):
        rows = pl.ds(pl.multiple_of(64 * k, 64), 64)
        out[k, :, pl.ds(0, 128)] = o32[0, rows].astype(BF16)
        out[k, :, pl.ds(128, 64)] = o32[1, rows, pl.ds(0, 64)].astype(BF16)
        return carry

    lax.fori_loop(0, HC, narrow, 0)
    move.wait()


def place_call(recv, enh):
    vmem = pl.BlockSpec(memory_space=pltpu.VMEM)
    any_ = pl.BlockSpec(memory_space=pl.ANY)
    return pl.pallas_call(
        place_kernel,
        out_shape=(
            jax.ShapeDtypeStruct((HC, 64, CAP), BF16),
            jax.ShapeDtypeStruct((HC, ROWS, COLS), BF16),
        ),
        in_specs=[vmem, any_],
        out_specs=(vmem, any_),
        scratch_shapes=[
            pltpu.VMEM((2, 2048, 128), F32),
            pltpu.VMEM((2, 2048, 128), F32),
            pltpu.SemaphoreType.DMA,
        ],
        compiler_params=pltpu.CompilerParams(vmem_limit_bytes=40 << 20),
        name="place_parents",
    )(recv, enh)


def on_device(features, tile_valid, parent_owner, w_first, w_second, w_merge):
    enh, recv = main_call(
        features, tile_valid, parent_owner.reshape(1, PAR), w_first, w_second,
        jnp.transpose(w_merge, (0, 2, 1)),
    )
    parents, enhanced = place_call(recv, enh)
    return (enhanced, jnp.transpose(parents, (0, 2, 1)))


def solution(mesh):
    return jax.shard_map(
        on_device,
        mesh=mesh,
        in_specs=(
            P("chan", "tiles", None),
            P("tiles", None),
            P("tiles"),
            P(None, "chan", None),
            P(None, "chan", None),
            P(None, None, "chan"),
        ),
        out_specs=(P("chan", "tiles", None), P("chan", "tiles", None)),
        check_vma=False,
    )
```

```python
import functools

import jax
import jax.numpy as jnp
from jax import lax
from jax.experimental import pallas as pl
from jax.experimental.pallas import tpu as pltpu
from jax.sharding import PartitionSpec as P

MESH = pl.DeviceIdType.MESH
F32, BF16 = jnp.float32, jnp.bfloat16
NT = 128
PLANE, LINE = 16, 8
ROWS = 128
COLS = 256
HALF = 64
CH = 64
HC = 32
PAR = 128
CAP = 192
EMPTY = 2.0**100


def dot(a, b):
    return jnp.dot(a, b, preferred_element_type=F32)


def dot_t(a, b):
    return lax.dot_general(a, b, (((1,), (1,)), ((), ())), preferred_element_type=F32)


def ones_at(shape, test):
    row = lax.broadcasted_iota(jnp.int32, shape, 0)
    col = lax.broadcasted_iota(jnp.int32, shape, 1)
    return jnp.where(test(row, col), 1.0, 0.0).astype(BF16)


def shifted_sum(z, shift, col):
    left = jnp.where(col >= shift, pltpu.roll(z[0:128], shift, 1), 0.0)
    right = jnp.where(col < COLS - shift, pltpu.roll(z[256:384], COLS - shift, 1), 0.0)
    return z[128:256] + left + right


def main_kernel(
    feat, valid_in, owner_in, w1raw, w2raw, wmraw,
    enh_out, recv,
    valid, owner, fv, f32t, x, h, e32, et, w1r, w2r, wmr, w1, w2, wm, near, mall, t1, tiles, tall, sel, s32, send,
    fsem, wsem, wsend, wrecv, xsend, xrecv, hsend, hrecv, bsem, esem, tsend, trecv, asem,
):
    t = lax.axis_index("tiles")
    c = lax.axis_index("chan")
    sib = 1 - c
    down = lax.rem(t + 1, NT)
    up = lax.rem(t + NT - 1, NT)
    base = HALF * c

    def remote(src, dst, ssem, rsem, tile, core):
        return pltpu.make_async_remote_copy(
            src, dst, ssem, rsem, device_id={"tiles": tile, "chan": core}, device_id_type=MESH
        )

    tx, tz, ty = t // 32, lax.rem(t // 4, LINE), lax.rem(t, 4)

    def in_plane(i):
        return lax.rem(tx + i // 4, 4) * 32 + tz * 4 + lax.rem(ty + i % 4, 4)

    def in_line(i):
        return tx * 32 + lax.rem(tz + i, LINE) * 4 + ty

    bar = pltpu.get_barrier_semaphore()
    near_by = [(t, sib), (down, 0), (down, 1), (up, 0), (up, 1)]
    groups = [[in_plane(i) for i in range(1, PLANE)], [in_line(i) for i in range(1, LINE)]]
    for tile, core in near_by + [(tile, c) for group in groups for tile in group]:
        pl.semaphore_signal(
            bar, inc=1, device_id={"tiles": tile, "chan": core}, device_id_type=MESH
        )

    def chunk_of(i, core):
        return lax.rem(i + 3 * (1 - core), 8)

    def load(i):
        rows = pl.ds(pl.multiple_of(16 * chunk_of(i, c), 16), 16)
        return pltpu.make_async_copy(feat.at[:, rows], fv.at[:, rows], fsem.at[i])

    small = [
        pltpu.make_async_copy(owner_in, owner, wsem.at[3]),
        pltpu.make_async_copy(valid_in, valid, wsem.at[4]),
    ]
    small[0].start()
    for i in range(8):
        load(i).start()
    small[1].start()
    my_ch = pl.ds(pl.multiple_of(c * HC, HC), HC)
    pieces = [(w1raw, w1r.at[:, my_ch]), (w2raw, w2r.at[:, my_ch]), (wmraw, wmr.at[:, my_ch])]
    w_own = [pltpu.make_async_copy(a, b, wsem.at[i]) for i, (a, b) in enumerate(pieces)]
    w_far = [remote(a, b, wsend.at[i], wrecv.at[i], t, sib) for i, (a, b) in enumerate(pieces)]
    w_far.append(remote(valid_in, near, wsend.at[3], wrecv.at[3], lax.rem(t + 1 - 2 * c + NT, NT), c))
    for copy in w_own:
        copy.start()

    def turn(i):
        load(i).wait()
        k = chunk_of(i, c)
        rows = pl.ds(pl.multiple_of(16 * k, 16), 16)
        for d2 in range(2):
            f32t[d2] = fv[:, rows, pl.ds(d2 * 128, 128)].astype(F32).reshape(512, 128)
        for r in range(16):
            for d2 in range(2):
                x[3 + 16 * k + r, my_ch, pl.ds(d2 * 128, 128)] = f32t[
                    d2, pl.ds(r, HC, stride=16), :
                ].astype(BF16)

    def x_copy(i, core):
        rows = pl.ds(3 + 16 * chunk_of(i, core), 16)
        part = x.at[rows, pl.ds(pl.multiple_of(core * HC, HC), HC)]
        return remote(part, part, xsend.at[i], xrecv.at[i], t, sib)

    turn(0)
    pl.semaphore_wait(bar, 5 + PLANE - 1 + LINE - 1)

    def signal_round(r):
        for tile in groups[r]:
            pl.semaphore_signal(
                bsem.at[r], inc=1, device_id={"tiles": tile, "chan": c}, device_id_type=MESH
            )

    signal_round(0)
    for copy in w_far:
        copy.start()
    x_copy(0, c).start()
    for i in range(1, 8):
        turn(i)
        if i < 5:
            x_copy(i, c).start()
    halo = [
        remote(x.at[pl.ds(ROWS, 3), my_ch], x.at[pl.ds(0, 3), my_ch], hsend.at[0], hrecv.at[c], down, 0),
        remote(x.at[pl.ds(3, 3), my_ch], x.at[pl.ds(131, 3), my_ch], hsend.at[1], hrecv.at[c], up, 1),
    ]
    for copy in halo:
        copy.start()

    small[0].wait()
    own_row = jnp.broadcast_to(owner[...], (PAR, PAR))
    own_col = jnp.transpose(own_row.astype(F32))
    row_id = lax.broadcasted_iota(jnp.int32, (PAR, PAR), 0)
    col_id = lax.broadcasted_iota(jnp.int32, (PAR, PAR), 1)
    before = jnp.where((own_col == own_row.astype(F32)) & (row_id < col_id), 1.0, 0.0)
    rank = jnp.sum(before, axis=0, keepdims=True)
    for k in range(2):
        hit = (row_id == own_row) & (jnp.broadcast_to(rank, (PAR, PAR)) == float(k))
        sel[pl.ds(k * PAR, PAR)] = jnp.where(hit, 1.0, 0.0).astype(BF16)

    for copy in w_own + small[1:]:
        copy.wait()
    for copy in w_far:
        copy.wait_recv()
    for raw, out in ((w1r, w1), (w2r, w2)):
        for first in range(2):
            rows = []
            for b in range(3):
                total = jnp.zeros((CH, 256), F32)
                for a in range(3):
                    place = ones_at((CH, 256), lambda i, j, s=a + first: j == i + CH * s)
                    total = total + dot(raw[3 * a + b], place)
                out[2 * b + first] = total.astype(BF16)
    for tr in range(4):
        place = ones_at((CH, 256), lambda i, j, tr=tr: j == (i // HC) * 128 + tr * HC + i % HC)
        for a in range(2):
            for b in range(2):
                wm[b * 8 + tr * 2 + a] = dot(wmr[2 * a + b], place).astype(BF16)
    spread = ones_at((32, COLS), lambda i, j: i == j // 8)
    mine = dot(valid[...].astype(F32).astype(BF16), spread)
    other = dot(near[...].astype(F32).astype(BF16), spread)
    inside_up = jnp.where(t > 0, 1.0, 0.0).astype(F32)
    inside_down = jnp.where(t < NT - 1, 1.0, 0.0).astype(F32)
    mall[0] = jnp.broadcast_to(other[15:16], (8, COLS)) * inside_up
    mall[17] = jnp.broadcast_to(other[0:1], (8, COLS)) * inside_down
    for i in range(16):
        mall[i + 1] = jnp.broadcast_to(mine[i : i + 1], (8, COLS))

    col = lax.broadcasted_iota(jnp.int32, (128, COLS), 1)

    def conv_one(j):
        m = lax.rem(j + 2 * (1 - c), 34)
        z = dot(w1[...].reshape(384, 256), x[pl.ds(base + 2 * m, 4)].reshape(256, COLS))
        out = shifted_sum(z, 1, col).reshape(16, 8, COLS) * mall[8 * c + (m + 3) // 4][None]
        out = jnp.maximum(out, 0.0).reshape(2, CH, COLS).astype(BF16)
        h[0, m] = out[0]
        h[1, m] = out[1]

    def phase_of_eight(phase, carry):
        x_copy(phase + 1, sib).wait_recv()
        for u in range(8):
            conv_one(8 * phase + u)
        return carry

    x_copy(0, sib).wait_recv()
    lax.fori_loop(0, 4, phase_of_eight, 0)

    edge = x.at[pl.ds(131 * c, 3), pl.ds(0, HC)]
    for k in range(2):
        pltpu.make_async_copy(edge, edge, hrecv.at[k]).wait()

    @pl.when((t == 0) & (c == 0))
    def _():
        x[pl.ds(0, 3)] = jnp.zeros((3, CH, COLS), BF16)

    @pl.when((t == NT - 1) & (c == 1))
    def _():
        x[pl.ds(131, 3)] = jnp.zeros((3, CH, COLS), BF16)

    conv_one(32)
    conv_one(33)
    pl.semaphore_wait(bsem.at[0], PLANE - 1)
    signal_round(1)

    perm = ones_at((256, 256), lambda i, j: j == 16 * (i % 16) + 2 * (i // 16 % 8) + i // 128)

    def conv_two(q):
        for n2 in range(2):
            n = 2 * q + n2
            rows = [None] * 4
            for p in range(2):
                z = dot(w2[...].reshape(384, 256), h[p, pl.ds(2 * n, 4)].reshape(256, COLS))
                out = shifted_sum(z, 2, col).reshape(2, CH, COLS)
                for i in range(2):
                    r = 4 * n + p + 2 * i
                    row = (out[i] + x[base + r + 3].astype(F32)).reshape(8, 8, COLS)
                    row = (row * mall[1 + 8 * c + q][None]).reshape(CH, COLS)
                    for d2 in range(2):
                        e32[d2, pl.ds(pl.multiple_of(r * CH, CH), CH)] = row[
                            :, d2 * 128 : d2 * 128 + 128
                        ]
                    rows[p + 2 * i] = row.astype(BF16)
            turned = dot_t(perm, jnp.concatenate(rows, axis=0)).astype(BF16)
            t1[q, :, pl.ds(n2 * 256, 256)] = turned[0:128]
            t1[q, :, pl.ds(512 + n2 * 256, 256)] = turned[128:256]

    def pair_of_two(k, carry):
        conv_two(2 * k)
        conv_two(2 * k + 1)
        return carry

    my_par = [pl.ds(pl.multiple_of(base + 32 * i, 32), 32) for i in range(2)]
    half = [pl.ds(32 * i, 32) for i in range(2)]
    t_own = [
        pltpu.make_async_copy(tiles.at[c, half[i]], tall.at[my_par[i]], wsem.at[i]) for i in range(2)
    ]
    t_far = [
        remote(tiles.at[sib, half[i]], tall.at[my_par[i]], tsend.at[i], trecv.at[i], t, sib)
        for i in range(2)
    ]
    for part in range(2):
        lax.fori_loop(2 * part, 2 * part + 2, pair_of_two, 0)
        four = t1[pl.ds(4 * part, 4)].reshape(512, 1024)
        merged = dot(four, wm[...].reshape(1024, 256)).astype(BF16)
        for q4 in range(4):
            g, tp = 2 * part + q4 // 2, q4 % 2
            for v in range(8):
                at = q4 * 128 + v * 16
                for k in range(2):
                    tiles[k, pl.ds(g * 16, 16), pl.ds((v * 2 + tp) * 128, 128)] = merged[
                        at : at + 16, k * 128 : k * 128 + 128
                    ]
        t_far[part].start()
        t_own[part].start()
    filled = jnp.sum(sel[...].astype(F32), axis=1, keepdims=True)
    pl.semaphore_wait(bsem.at[1], LINE - 1)
    for copy in t_own + t_far:
        copy.wait()

    for v in range(8):
        out = dot(sel[...], tall[:, pl.ds(v * 256, 256)])
        if v == 0:
            out = jnp.where(jnp.broadcast_to(filled, (256, 256)) > 0.5, out, EMPTY)
        for k in range(2):
            for d2 in range(2):
                s32[d2, pl.ds(v * 2 + k, 128, stride=16), :] = out[
                    k * 128 : k * 128 + 128, d2 * 128 : d2 * 128 + 128
                ]

    def deliver(i, carry):
        eight = lax.rem(t // 8 + i, NT // 8)
        for d2 in range(2):
            part = s32[d2, pl.ds(pl.multiple_of(128 * eight, 128), 128)]
            send[pl.ds(8 * eight, 8), :, pl.ds(d2 * 128, 128)] = part.astype(BF16).reshape(8, 16, 128)
        for k in range(8):
            d = 8 * eight + lax.rem(t + k, 8)

            @pl.when(d != t)
            def _():
                remote(send.at[d], recv.at[t], asem.at[0], asem.at[1], d, c).start()

        return carry

    lax.fori_loop(0, NT // 8, deliver, 0)
    own = pltpu.make_async_copy(send.at[t], recv.at[t], wsem.at[1])
    own.start()

    def back(k, carry):
        for d2 in range(2):
            et[k, :, pl.ds(d2 * 128, 128)] = e32[d2, pl.ds(k, HALF, stride=CH), :].astype(BF16)
        return carry

    lax.fori_loop(0, CH, back, 0)
    my_rows = pl.ds(pl.multiple_of(base, HALF), HALF)
    e_own = pltpu.make_async_copy(et.at[my_ch], enh_out.at[:, my_rows], wsem.at[2])
    e_far = remote(
        et.at[pl.ds(pl.multiple_of(sib * HC, HC), HC)], enh_out.at[:, my_rows],
        esem.at[0], esem.at[1], t, sib,
    )
    e_far.start()
    e_own.start()
    for copy in w_far + halo:
        copy.wait_send()
    for i in range(5):
        x_copy(i, c).wait_send()
    own.wait()
    e_own.wait()
    e_far.wait()
    others = recv.at[pl.ds(0, NT - 1)]
    gone = send.at[pl.ds(0, NT - 1)]
    pltpu.make_async_copy(gone, gone, asem.at[0]).wait()
    pltpu.make_async_copy(others, others, asem.at[1]).wait()


def main_call(feat, valid, owner, w1raw, w2raw, wmraw):
    any_ = pl.BlockSpec(memory_space=pl.ANY)
    dma = pltpu.SemaphoreType.DMA
    return pl.pallas_call(
        main_kernel,
        out_shape=(
            jax.ShapeDtypeStruct((HC, ROWS, COLS), BF16),
            jax.ShapeDtypeStruct((NT, 16, 256), BF16),
        ),
        in_specs=[pl.BlockSpec(memory_space=pltpu.HBM)] * 6,
        out_specs=(any_, any_),
        scratch_shapes=[
            pltpu.VMEM((16, 32), jnp.int32),
            pltpu.VMEM((1, PAR), jnp.int32),
            pltpu.VMEM((HC, ROWS, COLS), BF16),
            pltpu.VMEM((2, 512, 128), F32),
            pltpu.VMEM((134, CH, COLS), BF16),
            pltpu.VMEM((2, 34, CH, COLS), BF16),
            pltpu.VMEM((2, HALF * CH, 128), F32),
            pltpu.VMEM((CH, HALF, COLS), BF16),
            pltpu.VMEM((9, CH, CH), BF16),
            pltpu.VMEM((9, CH, CH), BF16),
            pltpu.VMEM((4, CH, CH), BF16),
            pltpu.VMEM((6, CH, 256), BF16),
            pltpu.VMEM((6, CH, 256), BF16),
            pltpu.VMEM((16, CH, 256), BF16),
            pltpu.VMEM((16, 32), jnp.int32),
            pltpu.VMEM((18, 8, COLS), F32),
            pltpu.VMEM((8, 128, 1024), BF16),
            pltpu.VMEM((2, HALF, 2048), BF16),
            pltpu.VMEM((PAR, 2048), BF16),
            pltpu.VMEM((256, PAR), BF16),
            pltpu.VMEM((2, 2048, 128), F32),
            pltpu.VMEM((NT, 16, 256), BF16),
            dma((8,)),
            dma((5,)),
            dma((4,)),
            dma((4,)),
            dma((5,)),
            dma((5,)),
            dma((2,)),
            dma((2,)),
            pltpu.SemaphoreType.REGULAR((2,)),
            dma((2,)),
            dma((2,)),
            dma((2,)),
            dma((2,)),
        ],
        compiler_params=pltpu.CompilerParams(
            collective_id=0, has_side_effects=True, vmem_limit_bytes=60 << 20
        ),
        name="convs_and_exchange",
    )(feat, valid, owner, w1raw, w2raw, wmraw)


def place_kernel(recv, enh, out, enh_out, got16, r32, o, hop, sem, rsem):
    parts = [pl.ds(8 * i, 8) for i in range(4)]
    ins = [pltpu.make_async_copy(enh.at[p], hop.at[p], sem.at[i]) for i, p in enumerate(parts)]
    outs = [pltpu.make_async_copy(hop.at[p], enh_out.at[p], sem.at[i]) for i, p in enumerate(parts)]
    some = [
        pltpu.make_async_copy(recv.at[pl.ds(32 * i, 32)], got16.at[pl.ds(32 * i, 32)], rsem.at[i])
        for i in range(4)
    ]
    for copy in some + ins:
        copy.start()

    for first in range(0, NT, 32):
        some[first // 32].wait()

        def widen(i, carry):
            for d2 in range(2):
                part = got16[pl.ds(8 * i, 8), :, pl.ds(d2 * 128, 128)].reshape(128, 128)
                r32[d2, pl.ds(pl.multiple_of(128 * i, 128), 128)] = part.astype(F32)
            return carry

        lax.fori_loop(first // 8, first // 8 + 4, widen, 0)
    here = [jnp.where(r32[0, pl.ds(k, 128, stride=16), :] < EMPTY, 1.0, 0.0) for k in range(2)]
    count = dot_t(ones_at((8, NT), lambda i, j: j == 0), (here[0] + here[1]).astype(BF16))
    start = dot(count.astype(BF16), ones_at((NT, NT), lambda i, j: i < j))
    slot = lax.broadcasted_iota(jnp.int32, (CAP, NT), 0).astype(F32)
    count = jnp.broadcast_to(count[0:1], (CAP, NT))
    start = jnp.broadcast_to(start[0:1], (CAP, NT))
    pick = jnp.concatenate(
        [
            jnp.where((slot == start + float(k)) & (count > float(k)), 1.0, 0.0)
            for k in range(2)
        ],
        axis=1,
    ).astype(BF16)
    by_four = ones_at((256, 256), lambda i, j: j == i % 32 // 4 * 32 + i // 32 * 4 + i % 4)
    for v in range(8):
        got = jnp.concatenate(
            [
                jnp.concatenate(
                    [r32[d2, pl.ds(v * 2 + k, 128, stride=16), :] for d2 in range(2)], axis=1
                )
                for k in range(2)
            ],
            axis=0,
        ).astype(BF16)
        o[v] = dot(dot(pick, got).astype(BF16), by_four).astype(BF16)
    for first, second in zip(ins, outs):
        first.wait()
        second.start()
    turn = ones_at((256, 256), lambda i, j: j == i % 8 * 32 + i // 8 % 8 * 4 + i // 64)
    lane = lax.broadcasted_iota(jnp.int32, (CAP, 128), 1) // 32
    for q in range(8):
        w, pos = q // 4, q % 4
        halves = []
        for hv in range(2):
            acc = jnp.zeros((CAP, 128), BF16)
            for i in range(4):
                part = o[hv * 4 + i, :, pl.ds(w * 128, 128)]
                if i != pos:
                    part = pltpu.roll(part, (32 * (i - pos)) % 128, 1)
                acc = jnp.where(lane == i, part, acc)
            halves.append(acc)
        last = dot_t(turn, jnp.concatenate(halves, axis=1)).astype(BF16)
        for i in range(4):
            out[q * 4 + i] = last[i * 64 : i * 64 + 64]
    for copy in outs:
        copy.wait()


def place_call(recv, enh):
    vmem = pl.BlockSpec(memory_space=pltpu.VMEM)
    any_ = pl.BlockSpec(memory_space=pl.ANY)
    return pl.pallas_call(
        place_kernel,
        out_shape=(
            jax.ShapeDtypeStruct((HC, 64, CAP), BF16),
            jax.ShapeDtypeStruct((HC, ROWS, COLS), BF16),
        ),
        in_specs=[any_, any_],
        out_specs=(vmem, any_),
        scratch_shapes=[
            pltpu.VMEM((NT, 16, 256), BF16),
            pltpu.VMEM((2, 2048, 128), F32),
            pltpu.VMEM((8, CAP, 256), BF16),
            pltpu.VMEM((HC, ROWS, COLS), BF16),
            pltpu.SemaphoreType.DMA((4,)),
            pltpu.SemaphoreType.DMA((4,)),
        ],
        compiler_params=pltpu.CompilerParams(vmem_limit_bytes=60 << 20),
        name="place_parents",
    )(recv, enh)


def on_device(features, tile_valid, parent_owner, w_first, w_second, w_merge):
    enh, recv = main_call(
        features, tile_valid, parent_owner.reshape(1, PAR), w_first, w_second,
        jnp.transpose(w_merge, (0, 2, 1)),
    )
    parents, enhanced = place_call(recv, enh)
    return (enhanced, jnp.transpose(parents, (0, 2, 1)))


def solution(mesh):
    return jax.shard_map(
        on_device,
        mesh=mesh,
        in_specs=(
            P("chan", "tiles", None),
            P("tiles", None),
            P("tiles"),
            P(None, "chan", None),
            P(None, "chan", None),
            P(None, None, "chan"),
        ),
        out_specs=(P("chan", "tiles", None), P("chan", "tiles", None)),
        check_vma=False,
    )
```

```python
import functools

import jax
import jax.numpy as jnp
from jax import lax
from jax.experimental import pallas as pl
from jax.experimental.pallas import tpu as pltpu
from jax.sharding import PartitionSpec as P

MESH = pl.DeviceIdType.MESH
F32, BF16 = jnp.float32, jnp.bfloat16
NT = 128
PLANE, LINE = 16, 8
ROWS = 128
COLS = 256
HALF = 64
CH = 64
HC = 32
PAR = 128
CAP = 192
EMPTY = 2.0**100


def dot(a, b):
    return jnp.dot(a, b, preferred_element_type=F32)


def dot_t(a, b):
    return lax.dot_general(a, b, (((1,), (1,)), ((), ())), preferred_element_type=F32)


def ones_at(shape, test):
    row = lax.broadcasted_iota(jnp.int32, shape, 0)
    col = lax.broadcasted_iota(jnp.int32, shape, 1)
    return jnp.where(test(row, col), 1.0, 0.0).astype(BF16)


def shifted_sum(z, shift, col):
    left = jnp.where(col >= shift, pltpu.roll(z[0:128], shift, 1), 0.0)
    right = jnp.where(col < COLS - shift, pltpu.roll(z[256:384], COLS - shift, 1), 0.0)
    return z[128:256] + left + right


def main_kernel(
    feat, valid_in, owner_in, w1raw, w2raw, wmraw,
    enh_out, recv,
    valid, owner, fv, f32t, x, h, e32, et, w1r, w2r, wmr, w1, w2, wm, near, mall, t1, tiles, tall, sel, s32, send,
    fsem, wsem, wsend, wrecv, xsend, xrecv, hsend, hrecv, bsem, esem, tsend, trecv, asem,
):
    t = lax.axis_index("tiles")
    c = lax.axis_index("chan")
    sib = 1 - c
    down = lax.rem(t + 1, NT)
    up = lax.rem(t + NT - 1, NT)
    base = HALF * c

    def remote(src, dst, ssem, rsem, tile, core):
        return pltpu.make_async_remote_copy(
            src, dst, ssem, rsem, device_id={"tiles": tile, "chan": core}, device_id_type=MESH
        )

    tx, tz, ty = t // 32, lax.rem(t // 4, LINE), lax.rem(t, 4)

    def in_plane(i):
        return lax.rem(tx + i // 4, 4) * 32 + tz * 4 + lax.rem(ty + i % 4, 4)

    def in_line(i):
        return tx * 32 + lax.rem(tz + i, LINE) * 4 + ty

    bar = pltpu.get_barrier_semaphore()
    near_by = [(t, sib), (down, 0), (down, 1), (up, 0), (up, 1)]
    groups = [[in_plane(i) for i in range(1, PLANE)], [in_line(i) for i in range(1, LINE)]]
    for tile, core in near_by + [(tile, c) for group in groups for tile in group]:
        pl.semaphore_signal(
            bar, inc=1, device_id={"tiles": tile, "chan": core}, device_id_type=MESH
        )

    def chunk_of(i, core):
        return lax.rem(i + 3 * (1 - core), 8)

    def load(i):
        rows = pl.ds(pl.multiple_of(16 * chunk_of(i, c), 16), 16)
        return pltpu.make_async_copy(feat.at[:, rows], fv.at[:, rows], fsem.at[i])

    small = [
        pltpu.make_async_copy(owner_in, owner, wsem.at[3]),
        pltpu.make_async_copy(valid_in, valid, wsem.at[4]),
    ]
    small[0].start()
    for i in range(8):
        load(i).start()
    small[1].start()
    my_ch = pl.ds(pl.multiple_of(c * HC, HC), HC)
    pieces = [(w1raw, w1r.at[:, my_ch]), (w2raw, w2r.at[:, my_ch]), (wmraw, wmr.at[:, my_ch])]
    w_own = [pltpu.make_async_copy(a, b, wsem.at[i]) for i, (a, b) in enumerate(pieces)]
    w_far = [remote(a, b, wsend.at[i], wrecv.at[i], t, sib) for i, (a, b) in enumerate(pieces)]
    w_far.append(remote(valid_in, near, wsend.at[3], wrecv.at[3], lax.rem(t + 1 - 2 * c + NT, NT), c))
    for copy in w_own:
        copy.start()

    def turn(i):
        load(i).wait()
        k = chunk_of(i, c)
        rows = pl.ds(pl.multiple_of(16 * k, 16), 16)
        for d2 in range(2):
            f32t[d2] = fv[:, rows, pl.ds(d2 * 128, 128)].astype(F32).reshape(512, 128)
        for r in range(16):
            for d2 in range(2):
                x[3 + 16 * k + r, my_ch, pl.ds(d2 * 128, 128)] = f32t[
                    d2, pl.ds(r, HC, stride=16), :
                ].astype(BF16)

    def x_copy(i, core):
        rows = pl.ds(3 + 16 * chunk_of(i, core), 16)
        part = x.at[rows, pl.ds(pl.multiple_of(core * HC, HC), HC)]
        return remote(part, part, xsend.at[i], xrecv.at[i], t, sib)

    pl.semaphore_wait(bar, 5 + PLANE - 1 + LINE - 1)

    def signal_round(r):
        for tile in groups[r]:
            pl.semaphore_signal(
                bsem.at[r], inc=1, device_id={"tiles": tile, "chan": c}, device_id_type=MESH
            )

    for copy in w_far:
        copy.start()
    turn(0)
    x_copy(0, c).start()
    signal_round(0)
    for i in range(1, 8):
        turn(i)
        if i < 5:
            x_copy(i, c).start()
    halo = [
        remote(x.at[pl.ds(ROWS, 3), my_ch], x.at[pl.ds(0, 3), my_ch], hsend.at[0], hrecv.at[c], down, 0),
        remote(x.at[pl.ds(3, 3), my_ch], x.at[pl.ds(131, 3), my_ch], hsend.at[1], hrecv.at[c], up, 1),
    ]
    for copy in halo:
        copy.start()

    for copy in w_own + small[1:]:
        copy.wait()
    for copy in w_far:
        copy.wait_recv()
    for raw, out in ((w1r, w1), (w2r, w2)):
        for first in range(2):
            rows = []
            for b in range(3):
                total = jnp.zeros((CH, 256), F32)
                for a in range(3):
                    place = ones_at((CH, 256), lambda i, j, s=a + first: j == i + CH * s)
                    total = total + dot(raw[3 * a + b], place)
                out[2 * b + first] = total.astype(BF16)
    for tr in range(4):
        place = ones_at((CH, 256), lambda i, j, tr=tr: j == (i // HC) * 128 + tr * HC + i % HC)
        for a in range(2):
            for b in range(2):
                wm[b * 8 + tr * 2 + a] = dot(wmr[2 * a + b], place).astype(BF16)
    spread = ones_at((32, COLS), lambda i, j: i == j // 8)
    mine = dot(valid[...].astype(F32).astype(BF16), spread)
    other = dot(near[...].astype(F32).astype(BF16), spread)
    inside_up = jnp.where(t > 0, 1.0, 0.0).astype(F32)
    inside_down = jnp.where(t < NT - 1, 1.0, 0.0).astype(F32)
    mall[0] = jnp.broadcast_to(other[15:16], (8, COLS)) * inside_up
    mall[17] = jnp.broadcast_to(other[0:1], (8, COLS)) * inside_down
    for i in range(16):
        mall[i + 1] = jnp.broadcast_to(mine[i : i + 1], (8, COLS))

    col = lax.broadcasted_iota(jnp.int32, (128, COLS), 1)

    def conv_one(j):
        m = lax.rem(j + 2 * (1 - c), 34)
        z = dot(w1[...].reshape(384, 256), x[pl.ds(base + 2 * m, 4)].reshape(256, COLS))
        out = shifted_sum(z, 1, col).reshape(16, 8, COLS) * mall[8 * c + (m + 3) // 4][None]
        out = jnp.maximum(out, 0.0).reshape(2, CH, COLS).astype(BF16)
        h[0, m] = out[0]
        h[1, m] = out[1]

    def phase_of_eight(phase, carry):
        x_copy(phase + 1, sib).wait_recv()
        for u in range(8):
            conv_one(8 * phase + u)
        return carry

    x_copy(0, sib).wait_recv()
    lax.fori_loop(0, 4, phase_of_eight, 0)

    edge = x.at[pl.ds(131 * c, 3), pl.ds(0, HC)]
    for k in range(2):
        pltpu.make_async_copy(edge, edge, hrecv.at[k]).wait()

    @pl.when((t == 0) & (c == 0))
    def _():
        x[pl.ds(0, 3)] = jnp.zeros((3, CH, COLS), BF16)

    @pl.when((t == NT - 1) & (c == 1))
    def _():
        x[pl.ds(131, 3)] = jnp.zeros((3, CH, COLS), BF16)

    conv_one(32)
    conv_one(33)
    pl.semaphore_wait(bsem.at[0], PLANE - 1)
    signal_round(1)

    perm = ones_at((256, 256), lambda i, j: j == 16 * (i % 16) + 2 * (i // 16 % 8) + i // 128)

    def conv_two(q):
        for n2 in range(2):
            n = 2 * q + n2
            rows = [None] * 4
            for p in range(2):
                z = dot(w2[...].reshape(384, 256), h[p, pl.ds(2 * n, 4)].reshape(256, COLS))
                out = shifted_sum(z, 2, col).reshape(2, CH, COLS)
                for i in range(2):
                    r = 4 * n + p + 2 * i
                    row = (out[i] + x[base + r + 3].astype(F32)).reshape(8, 8, COLS)
                    row = (row * mall[1 + 8 * c + q][None]).reshape(CH, COLS)
                    for d2 in range(2):
                        e32[d2, pl.ds(pl.multiple_of(r * CH, CH), CH)] = row[
                            :, d2 * 128 : d2 * 128 + 128
                        ]
                    rows[p + 2 * i] = row.astype(BF16)
            turned = dot_t(perm, jnp.concatenate(rows, axis=0)).astype(BF16)
            t1[q, :, pl.ds(n2 * 256, 256)] = turned[0:128]
            t1[q, :, pl.ds(512 + n2 * 256, 256)] = turned[128:256]

    def pair_of_two(k, carry):
        conv_two(2 * k)
        conv_two(2 * k + 1)
        return carry

    my_par = [pl.ds(pl.multiple_of(base + 32 * i, 32), 32) for i in range(2)]
    half = [pl.ds(32 * i, 32) for i in range(2)]
    t_own = [
        pltpu.make_async_copy(tiles.at[c, half[i]], tall.at[my_par[i]], wsem.at[i]) for i in range(2)
    ]
    t_far = [
        remote(tiles.at[sib, half[i]], tall.at[my_par[i]], tsend.at[i], trecv.at[i], t, sib)
        for i in range(2)
    ]
    for part in range(2):
        lax.fori_loop(2 * part, 2 * part + 2, pair_of_two, 0)
        four = t1[pl.ds(4 * part, 4)].reshape(512, 1024)
        merged = dot(four, wm[...].reshape(1024, 256)).astype(BF16)
        for q4 in range(4):
            g, tp = 2 * part + q4 // 2, q4 % 2
            for v in range(8):
                at = q4 * 128 + v * 16
                for k in range(2):
                    tiles[k, pl.ds(g * 16, 16), pl.ds((v * 2 + tp) * 128, 128)] = merged[
                        at : at + 16, k * 128 : k * 128 + 128
                    ]
        t_far[part].start()
        t_own[part].start()
    small[0].wait()
    own_row = jnp.broadcast_to(owner[...], (PAR, PAR))
    own_col = jnp.transpose(own_row.astype(F32))
    row_id = lax.broadcasted_iota(jnp.int32, (PAR, PAR), 0)
    col_id = lax.broadcasted_iota(jnp.int32, (PAR, PAR), 1)
    before = jnp.where((own_col == own_row.astype(F32)) & (row_id < col_id), 1.0, 0.0)
    rank = jnp.sum(before, axis=0, keepdims=True)
    for k in range(2):
        hit = (row_id == own_row) & (jnp.broadcast_to(rank, (PAR, PAR)) == float(k))
        sel[pl.ds(k * PAR, PAR)] = jnp.where(hit, 1.0, 0.0).astype(BF16)

    filled = jnp.sum(sel[...].astype(F32), axis=1, keepdims=True)
    pl.semaphore_wait(bsem.at[1], LINE - 1)
    for copy in t_own + t_far:
        copy.wait()

    for v in range(8):
        out = dot(sel[...], tall[:, pl.ds(v * 256, 256)])
        if v == 0:
            out = jnp.where(jnp.broadcast_to(filled, (256, 256)) > 0.5, out, EMPTY)
        for k in range(2):
            for d2 in range(2):
                s32[d2, pl.ds(v * 2 + k, 128, stride=16), :] = out[
                    k * 128 : k * 128 + 128, d2 * 128 : d2 * 128 + 128
                ]

    def deliver(i, carry):
        eight = lax.rem(t // 8 + i, NT // 8)
        for d2 in range(2):
            part = s32[d2, pl.ds(pl.multiple_of(128 * eight, 128), 128)]
            send[pl.ds(8 * eight, 8), :, pl.ds(d2 * 128, 128)] = part.astype(BF16).reshape(8, 16, 128)
        for k in range(8):
            d = 8 * eight + lax.rem(t + k, 8)

            @pl.when(d != t)
            def _():
                remote(send.at[d], recv.at[t], asem.at[0], asem.at[1], d, c).start()

        return carry

    lax.fori_loop(0, NT // 8, deliver, 0)
    own = pltpu.make_async_copy(send.at[t], recv.at[t], wsem.at[1])
    own.start()

    def back(k, carry):
        for d2 in range(2):
            et[k, :, pl.ds(d2 * 128, 128)] = e32[d2, pl.ds(k, HALF, stride=CH), :].astype(BF16)
        return carry

    lax.fori_loop(0, CH, back, 0)
    my_rows = pl.ds(pl.multiple_of(base, HALF), HALF)
    e_own = pltpu.make_async_copy(et.at[my_ch], enh_out.at[:, my_rows], wsem.at[2])
    e_far = remote(
        et.at[pl.ds(pl.multiple_of(sib * HC, HC), HC)], enh_out.at[:, my_rows],
        esem.at[0], esem.at[1], t, sib,
    )
    e_far.start()
    e_own.start()
    for copy in w_far + halo:
        copy.wait_send()
    for i in range(5):
        x_copy(i, c).wait_send()
    own.wait()
    e_own.wait()
    e_far.wait()
    others = recv.at[pl.ds(0, NT - 1)]
    gone = send.at[pl.ds(0, NT - 1)]
    pltpu.make_async_copy(gone, gone, asem.at[0]).wait()
    pltpu.make_async_copy(others, others, asem.at[1]).wait()


def main_call(feat, valid, owner, w1raw, w2raw, wmraw):
    any_ = pl.BlockSpec(memory_space=pl.ANY)
    dma = pltpu.SemaphoreType.DMA
    return pl.pallas_call(
        main_kernel,
        out_shape=(
            jax.ShapeDtypeStruct((HC, ROWS, COLS), BF16),
            jax.ShapeDtypeStruct((NT, 16, 256), BF16),
        ),
        in_specs=[pl.BlockSpec(memory_space=pltpu.HBM)] * 6,
        out_specs=(any_, any_),
        scratch_shapes=[
            pltpu.VMEM((16, 32), jnp.int32),
            pltpu.VMEM((1, PAR), jnp.int32),
            pltpu.VMEM((HC, ROWS, COLS), BF16),
            pltpu.VMEM((2, 512, 128), F32),
            pltpu.VMEM((134, CH, COLS), BF16),
            pltpu.VMEM((2, 34, CH, COLS), BF16),
            pltpu.VMEM((2, HALF * CH, 128), F32),
            pltpu.VMEM((CH, HALF, COLS), BF16),
            pltpu.VMEM((9, CH, CH), BF16),
            pltpu.VMEM((9, CH, CH), BF16),
            pltpu.VMEM((4, CH, CH), BF16),
            pltpu.VMEM((6, CH, 256), BF16),
            pltpu.VMEM((6, CH, 256), BF16),
            pltpu.VMEM((16, CH, 256), BF16),
            pltpu.VMEM((16, 32), jnp.int32),
            pltpu.VMEM((18, 8, COLS), F32),
            pltpu.VMEM((8, 128, 1024), BF16),
            pltpu.VMEM((2, HALF, 2048), BF16),
            pltpu.VMEM((PAR, 2048), BF16),
            pltpu.VMEM((256, PAR), BF16),
            pltpu.VMEM((2, 2048, 128), F32),
            pltpu.VMEM((NT, 16, 256), BF16),
            dma((8,)),
            dma((5,)),
            dma((4,)),
            dma((4,)),
            dma((5,)),
            dma((5,)),
            dma((2,)),
            dma((2,)),
            pltpu.SemaphoreType.REGULAR((2,)),
            dma((2,)),
            dma((2,)),
            dma((2,)),
            dma((2,)),
        ],
        compiler_params=pltpu.CompilerParams(
            collective_id=0, has_side_effects=True, vmem_limit_bytes=60 << 20
        ),
        name="convs_and_exchange",
    )(feat, valid, owner, w1raw, w2raw, wmraw)


def place_kernel(recv, enh, out, enh_out, got16, r32, o, hop, mine, sem, rsem, psem):
    parts = [pl.ds(8 * i, 8) for i in range(4)]
    ins = [pltpu.make_async_copy(enh.at[p], hop.at[p], sem.at[i]) for i, p in enumerate(parts)]
    outs = [pltpu.make_async_copy(hop.at[p], enh_out.at[p], sem.at[i]) for i, p in enumerate(parts)]
    some = [
        pltpu.make_async_copy(recv.at[pl.ds(32 * i, 32)], got16.at[pl.ds(32 * i, 32)], rsem.at[i])
        for i in range(4)
    ]
    for copy in some + ins:
        copy.start()

    for first in range(0, NT, 32):
        some[first // 32].wait()

        def widen(i, carry):
            for d2 in range(2):
                part = got16[pl.ds(8 * i, 8), :, pl.ds(d2 * 128, 128)].reshape(128, 128)
                r32[d2, pl.ds(pl.multiple_of(128 * i, 128), 128)] = part.astype(F32)
            return carry

        lax.fori_loop(first // 8, first // 8 + 4, widen, 0)
    here = [jnp.where(r32[0, pl.ds(k, 128, stride=16), :] < EMPTY, 1.0, 0.0) for k in range(2)]
    count = dot_t(ones_at((8, NT), lambda i, j: j == 0), (here[0] + here[1]).astype(BF16))
    start = dot(count.astype(BF16), ones_at((NT, NT), lambda i, j: i < j))
    slot = lax.broadcasted_iota(jnp.int32, (CAP, NT), 0).astype(F32)
    count = jnp.broadcast_to(count[0:1], (CAP, NT))
    start = jnp.broadcast_to(start[0:1], (CAP, NT))
    pick = jnp.concatenate(
        [
            jnp.where((slot == start + float(k)) & (count > float(k)), 1.0, 0.0)
            for k in range(2)
        ],
        axis=1,
    ).astype(BF16)
    by_four = ones_at((256, 256), lambda i, j: j == i % 32 // 4 * 32 + i // 32 * 4 + i % 4)
    for v in range(8):
        got = jnp.concatenate(
            [
                jnp.concatenate(
                    [r32[d2, pl.ds(v * 2 + k, 128, stride=16), :] for d2 in range(2)], axis=1
                )
                for k in range(2)
            ],
            axis=0,
        ).astype(BF16)
        o[v] = dot(dot(pick, got).astype(BF16), by_four).astype(BF16)
    for first, second in zip(ins, outs):
        first.wait()
        second.start()
    turn = ones_at((256, 256), lambda i, j: j == i % 8 * 32 + i // 8 % 8 * 4 + i // 64)
    lane = lax.broadcasted_iota(jnp.int32, (CAP, 128), 1) // 32
    for q in range(8):
        w, pos = q // 4, q % 4
        halves = []
        for hv in range(2):
            acc = jnp.zeros((CAP, 128), BF16)
            for i in range(4):
                part = o[hv * 4 + i, :, pl.ds(w * 128, 128)]
                if i != pos:
                    part = pltpu.roll(part, (32 * (i - pos)) % 128, 1)
                acc = jnp.where(lane == i, part, acc)
            halves.append(acc)
        last = dot_t(turn, jnp.concatenate(halves, axis=1)).astype(BF16)
        for i in range(4):
            mine[q * 4 + i] = last[i * 64 : i * 64 + 64]
        outs.append(
            pltpu.make_async_copy(mine.at[pl.ds(4 * q, 4)], out.at[pl.ds(4 * q, 4)], psem.at[q])
        )
        outs[-1].start()
    for copy in outs:
        copy.wait()


def place_call(recv, enh):
    any_ = pl.BlockSpec(memory_space=pl.ANY)
    return pl.pallas_call(
        place_kernel,
        out_shape=(
            jax.ShapeDtypeStruct((HC, 64, CAP), BF16),
            jax.ShapeDtypeStruct((HC, ROWS, COLS), BF16),
        ),
        in_specs=[any_, any_],
        out_specs=(any_, any_),
        scratch_shapes=[
            pltpu.VMEM((NT, 16, 256), BF16),
            pltpu.VMEM((2, 2048, 128), F32),
            pltpu.VMEM((8, CAP, 256), BF16),
            pltpu.VMEM((HC, ROWS, COLS), BF16),
            pltpu.VMEM((HC, 64, CAP), BF16),
            pltpu.SemaphoreType.DMA((4,)),
            pltpu.SemaphoreType.DMA((4,)),
            pltpu.SemaphoreType.DMA((8,)),
        ],
        compiler_params=pltpu.CompilerParams(vmem_limit_bytes=60 << 20),
        name="place_parents",
    )(recv, enh)


def on_device(features, tile_valid, parent_owner, w_first, w_second, w_merge):
    enh, recv = main_call(
        features, tile_valid, parent_owner.reshape(1, PAR), w_first, w_second,
        jnp.transpose(w_merge, (0, 2, 1)),
    )
    parents, enhanced = place_call(recv, enh)
    return (enhanced, jnp.transpose(parents, (0, 2, 1)))


def solution(mesh):
    return jax.shard_map(
        on_device,
        mesh=mesh,
        in_specs=(
            P("chan", "tiles", None),
            P("tiles", None),
            P("tiles"),
            P(None, "chan", None),
            P(None, "chan", None),
            P(None, None, "chan"),
        ),
        out_specs=(P("chan", "tiles", None), P("chan", "tiles", None)),
        check_vma=False,
    )
```

```python
import functools

import jax
import jax.numpy as jnp
from jax import lax
from jax.experimental import pallas as pl
from jax.experimental.pallas import tpu as pltpu
from jax.sharding import PartitionSpec as P

MESH = pl.DeviceIdType.MESH
F32, BF16 = jnp.float32, jnp.bfloat16
NT = 128
PLANE, LINE = 16, 8
ROWS = 128
COLS = 256
HALF = 64
CH = 64
HC = 32
PAR = 128
CAP = 192
EMPTY = 2.0**100


def dot(a, b):
    return jnp.dot(a, b, preferred_element_type=F32)


def dot_t(a, b):
    return lax.dot_general(a, b, (((1,), (1,)), ((), ())), preferred_element_type=F32)


def ones_at(shape, test):
    row = lax.broadcasted_iota(jnp.int32, shape, 0)
    col = lax.broadcasted_iota(jnp.int32, shape, 1)
    return jnp.where(test(row, col), 1.0, 0.0).astype(BF16)


def shifted_sum(z, shift, col):
    left = jnp.where(col >= shift, pltpu.roll(z[0:128], shift, 1), 0.0)
    right = jnp.where(col < COLS - shift, pltpu.roll(z[256:384], COLS - shift, 1), 0.0)
    return z[128:256] + left + right


def main_kernel(
    feat, valid_in, owner_in, w1raw, w2raw, wmraw,
    enh_out, recv,
    valid, owner, fv, f32t, x, h, e32, et, w1r, w2r, wmr, w1, w2, wm, near, mall, t1, tiles, tall, sel, s32, send,
    fsem, wsem, wsend, wrecv, xsend, xrecv, hsend, hrecv, bsem, esem, tsend, trecv, asem,
):
    t = lax.axis_index("tiles")
    c = lax.axis_index("chan")
    sib = 1 - c
    down = lax.rem(t + 1, NT)
    up = lax.rem(t + NT - 1, NT)
    base = HALF * c

    def remote(src, dst, ssem, rsem, tile, core):
        return pltpu.make_async_remote_copy(
            src, dst, ssem, rsem, device_id={"tiles": tile, "chan": core}, device_id_type=MESH
        )

    tx, tz, ty = t // 32, lax.rem(t // 4, LINE), lax.rem(t, 4)

    def in_plane(i):
        return lax.rem(tx + i // 4, 4) * 32 + tz * 4 + lax.rem(ty + i % 4, 4)

    def in_line(i):
        return tx * 32 + lax.rem(tz + i, LINE) * 4 + ty

    bar = pltpu.get_barrier_semaphore()
    near_by = [(t, sib), (down, 0), (down, 1), (up, 0), (up, 1)]
    groups = [[in_plane(i) for i in range(1, PLANE)], [in_line(i) for i in range(1, LINE)]]
    for tile, core in near_by + [(tile, c) for group in groups for tile in group]:
        pl.semaphore_signal(
            bar, inc=1, device_id={"tiles": tile, "chan": core}, device_id_type=MESH
        )

    def chunk_of(i, core):
        return lax.rem(i + 3 * (1 - core), 8)

    def load(i):
        rows = pl.ds(pl.multiple_of(16 * chunk_of(i, c), 16), 16)
        return pltpu.make_async_copy(feat.at[:, rows], fv.at[:, rows], fsem.at[i])

    small = [
        pltpu.make_async_copy(owner_in, owner, wsem.at[3]),
        pltpu.make_async_copy(valid_in, valid, wsem.at[4]),
    ]
    small[0].start()
    for i in range(8):
        load(i).start()
    small[1].start()
    my_ch = pl.ds(pl.multiple_of(c * HC, HC), HC)
    pieces = [(w1raw, w1r.at[:, my_ch]), (w2raw, w2r.at[:, my_ch]), (wmraw, wmr.at[:, my_ch])]
    w_own = [pltpu.make_async_copy(a, b, wsem.at[i]) for i, (a, b) in enumerate(pieces)]
    w_far = [remote(a, b, wsend.at[i], wrecv.at[i], t, sib) for i, (a, b) in enumerate(pieces)]
    w_far.append(remote(valid_in, near, wsend.at[3], wrecv.at[3], lax.rem(t + 1 - 2 * c + NT, NT), c))
    for copy in w_own:
        copy.start()

    def turn(i):
        load(i).wait()
        k = chunk_of(i, c)
        rows = pl.ds(pl.multiple_of(16 * k, 16), 16)
        for d2 in range(2):
            f32t[d2] = fv[:, rows, pl.ds(d2 * 128, 128)].astype(F32).reshape(512, 128)
        for r in range(16):
            for d2 in range(2):
                x[3 + 16 * k + r, my_ch, pl.ds(d2 * 128, 128)] = f32t[
                    d2, pl.ds(r, HC, stride=16), :
                ].astype(BF16)

    def x_copy(i, core):
        rows = pl.ds(3 + 16 * chunk_of(i, core), 16)
        part = x.at[rows, pl.ds(pl.multiple_of(core * HC, HC), HC)]
        return remote(part, part, xsend.at[i], xrecv.at[i], t, sib)

    pl.semaphore_wait(bar, 5 + PLANE - 1 + LINE - 1)

    def signal_round(r):
        for tile in groups[r]:
            pl.semaphore_signal(
                bsem.at[r], inc=1, device_id={"tiles": tile, "chan": c}, device_id_type=MESH
            )

    for copy in w_far:
        copy.start()
    turn(0)
    x_copy(0, c).start()
    signal_round(0)
    for i in range(1, 8):
        turn(i)
        if i < 5:
            x_copy(i, c).start()
    halo = [
        remote(x.at[pl.ds(ROWS, 3), my_ch], x.at[pl.ds(0, 3), my_ch], hsend.at[0], hrecv.at[c], down, 0),
        remote(x.at[pl.ds(3, 3), my_ch], x.at[pl.ds(131, 3), my_ch], hsend.at[1], hrecv.at[c], up, 1),
    ]
    for copy in halo:
        copy.start()

    for copy in w_own + small[1:]:
        copy.wait()
    for copy in w_far:
        copy.wait_recv()
    for raw, out in ((w1r, w1), (w2r, w2)):
        for first in range(2):
            rows = []
            for b in range(3):
                total = jnp.zeros((CH, 256), F32)
                for a in range(3):
                    place = ones_at((CH, 256), lambda i, j, s=a + first: j == i + CH * s)
                    total = total + dot(raw[3 * a + b], place)
                out[2 * b + first] = total.astype(BF16)
    for tr in range(4):
        place = ones_at((CH, 256), lambda i, j, tr=tr: j == (i // HC) * 128 + tr * HC + i % HC)
        for a in range(2):
            for b in range(2):
                wm[b * 8 + tr * 2 + a] = dot(wmr[2 * a + b], place).astype(BF16)
    spread = ones_at((32, COLS), lambda i, j: i == j // 8)
    mine = dot(valid[...].astype(F32).astype(BF16), spread)
    other = dot(near[...].astype(F32).astype(BF16), spread)
    inside_up = jnp.where(t > 0, 1.0, 0.0).astype(F32)
    inside_down = jnp.where(t < NT - 1, 1.0, 0.0).astype(F32)
    mall[0] = jnp.broadcast_to(other[15:16], (8, COLS)) * inside_up
    mall[17] = jnp.broadcast_to(other[0:1], (8, COLS)) * inside_down
    for i in range(16):
        mall[i + 1] = jnp.broadcast_to(mine[i : i + 1], (8, COLS))

    col = lax.broadcasted_iota(jnp.int32, (128, COLS), 1)

    def conv_one(j):
        m = lax.rem(j + 2 * (1 - c), 34)
        z = dot(w1[...].reshape(384, 256), x[pl.ds(base + 2 * m, 4)].reshape(256, COLS))
        out = shifted_sum(z, 1, col).reshape(16, 8, COLS) * mall[8 * c + (m + 3) // 4][None]
        out = jnp.maximum(out, 0.0).reshape(2, CH, COLS).astype(BF16)
        h[0, m] = out[0]
        h[1, m] = out[1]

    def phase_of_eight(phase, carry):
        x_copy(phase + 1, sib).wait_recv()
        for u in range(8):
            conv_one(8 * phase + u)
        return carry

    x_copy(0, sib).wait_recv()
    lax.fori_loop(0, 4, phase_of_eight, 0)

    edge = x.at[pl.ds(131 * c, 3), pl.ds(0, HC)]
    for k in range(2):
        pltpu.make_async_copy(edge, edge, hrecv.at[k]).wait()

    @pl.when((t == 0) & (c == 0))
    def _():
        x[pl.ds(0, 3)] = jnp.zeros((3, CH, COLS), BF16)

    @pl.when((t == NT - 1) & (c == 1))
    def _():
        x[pl.ds(131, 3)] = jnp.zeros((3, CH, COLS), BF16)

    conv_one(32)
    conv_one(33)
    pl.semaphore_wait(bsem.at[0], PLANE - 1)
    signal_round(1)

    perm = ones_at((256, 256), lambda i, j: j == 16 * (i % 16) + 2 * (i // 16 % 8) + i // 128)

    def conv_two(q):
        for n2 in range(2):
            n = 2 * q + n2
            rows = [None] * 4
            for p in range(2):
                z = dot(w2[...].reshape(384, 256), h[p, pl.ds(2 * n, 4)].reshape(256, COLS))
                out = shifted_sum(z, 2, col).reshape(2, CH, COLS)
                for i in range(2):
                    r = 4 * n + p + 2 * i
                    row = (out[i] + x[base + r + 3].astype(F32)).reshape(8, 8, COLS)
                    row = (row * mall[1 + 8 * c + q][None]).reshape(CH, COLS)
                    for d2 in range(2):
                        e32[d2, pl.ds(pl.multiple_of(r * CH, CH), CH)] = row[
                            :, d2 * 128 : d2 * 128 + 128
                        ]
                    rows[p + 2 * i] = row.astype(BF16)
            turned = dot_t(perm, jnp.concatenate(rows, axis=0)).astype(BF16)
            t1[q, :, pl.ds(n2 * 256, 256)] = turned[0:128]
            t1[q, :, pl.ds(512 + n2 * 256, 256)] = turned[128:256]

    def pair_of_two(k, carry):
        conv_two(2 * k)
        conv_two(2 * k + 1)
        return carry

    my_par = [
        pl.ds(pl.multiple_of(base, 16), 48), pl.ds(pl.multiple_of(base + 48, 16), 16)
    ]
    half = [pl.ds(0, 48), pl.ds(48, 16)]
    t_own = [
        pltpu.make_async_copy(tiles.at[c, half[i]], tall.at[my_par[i]], wsem.at[i]) for i in range(2)
    ]
    t_far = [
        remote(tiles.at[sib, half[i]], tall.at[my_par[i]], tsend.at[i], trecv.at[i], t, sib)
        for i in range(2)
    ]
    for part in range(2):
        lax.fori_loop(3 * part, 3 + part, pair_of_two, 0)
        count = 6 - 4 * part
        some = t1[pl.ds(6 * part, count)].reshape(128 * count, 1024)
        merged = dot(some, wm[...].reshape(1024, 256)).astype(BF16)
        for q4 in range(count):
            g, tp = 3 * part + q4 // 2, q4 % 2
            for v in range(8):
                at = q4 * 128 + v * 16
                for k in range(2):
                    tiles[k, pl.ds(g * 16, 16), pl.ds((v * 2 + tp) * 128, 128)] = merged[
                        at : at + 16, k * 128 : k * 128 + 128
                    ]
        t_far[part].start()
        t_own[part].start()
    small[0].wait()
    own_row = jnp.broadcast_to(owner[...], (PAR, PAR))
    own_col = jnp.transpose(own_row.astype(F32))
    row_id = lax.broadcasted_iota(jnp.int32, (PAR, PAR), 0)
    col_id = lax.broadcasted_iota(jnp.int32, (PAR, PAR), 1)
    before = jnp.where((own_col == own_row.astype(F32)) & (row_id < col_id), 1.0, 0.0)
    rank = jnp.sum(before, axis=0, keepdims=True)
    for k in range(2):
        hit = (row_id == own_row) & (jnp.broadcast_to(rank, (PAR, PAR)) == float(k))
        sel[pl.ds(k * PAR, PAR)] = jnp.where(hit, 1.0, 0.0).astype(BF16)

    filled = jnp.sum(sel[...].astype(F32), axis=1, keepdims=True)
    pl.semaphore_wait(bsem.at[1], LINE - 1)
    for copy in t_own + t_far:
        copy.wait()

    for v in range(8):
        out = dot(sel[...], tall[:, pl.ds(v * 256, 256)])
        if v == 0:
            out = jnp.where(jnp.broadcast_to(filled, (256, 256)) > 0.5, out, EMPTY)
        for k in range(2):
            for d2 in range(2):
                s32[d2, pl.ds(v * 2 + k, 128, stride=16), :] = out[
                    k * 128 : k * 128 + 128, d2 * 128 : d2 * 128 + 128
                ]

    def deliver(i, carry):
        eight = lax.rem(t // 8 + i, NT // 8)
        for d2 in range(2):
            part = s32[d2, pl.ds(pl.multiple_of(128 * eight, 128), 128)]
            send[pl.ds(8 * eight, 8), :, pl.ds(d2 * 128, 128)] = part.astype(BF16).reshape(8, 16, 128)
        for k in range(8):
            d = 8 * eight + lax.rem(t + k, 8)

            @pl.when(d != t)
            def _():
                remote(send.at[d], recv.at[t], asem.at[0], asem.at[1], d, c).start()

        return carry

    lax.fori_loop(0, NT // 8, deliver, 0)
    own = pltpu.make_async_copy(send.at[t], recv.at[t], wsem.at[1])
    own.start()

    def back(k, carry):
        for d2 in range(2):
            et[k, :, pl.ds(d2 * 128, 128)] = e32[d2, pl.ds(k, HALF, stride=CH), :].astype(BF16)
        return carry

    lax.fori_loop(0, CH, back, 0)
    my_rows = pl.ds(pl.multiple_of(base, HALF), HALF)
    e_own = pltpu.make_async_copy(et.at[my_ch], enh_out.at[:, my_rows], wsem.at[2])
    e_far = remote(
        et.at[pl.ds(pl.multiple_of(sib * HC, HC), HC)], enh_out.at[:, my_rows],
        esem.at[0], esem.at[1], t, sib,
    )
    e_far.start()
    e_own.start()
    for copy in w_far + halo:
        copy.wait_send()
    for i in range(5):
        x_copy(i, c).wait_send()
    own.wait()
    e_own.wait()
    e_far.wait()
    others = recv.at[pl.ds(0, NT - 1)]
    gone = send.at[pl.ds(0, NT - 1)]
    pltpu.make_async_copy(gone, gone, asem.at[0]).wait()
    pltpu.make_async_copy(others, others, asem.at[1]).wait()


def main_call(feat, valid, owner, w1raw, w2raw, wmraw):
    any_ = pl.BlockSpec(memory_space=pl.ANY)
    dma = pltpu.SemaphoreType.DMA
    return pl.pallas_call(
        main_kernel,
        out_shape=(
            jax.ShapeDtypeStruct((HC, ROWS, COLS), BF16),
            jax.ShapeDtypeStruct((NT, 16, 256), BF16),
        ),
        in_specs=[pl.BlockSpec(memory_space=pltpu.HBM)] * 6,
        out_specs=(any_, any_),
        scratch_shapes=[
            pltpu.VMEM((16, 32), jnp.int32),
            pltpu.VMEM((1, PAR), jnp.int32),
            pltpu.VMEM((HC, ROWS, COLS), BF16),
            pltpu.VMEM((2, 512, 128), F32),
            pltpu.VMEM((134, CH, COLS), BF16),
            pltpu.VMEM((2, 34, CH, COLS), BF16),
            pltpu.VMEM((2, HALF * CH, 128), F32),
            pltpu.VMEM((CH, HALF, COLS), BF16),
            pltpu.VMEM((9, CH, CH), BF16),
            pltpu.VMEM((9, CH, CH), BF16),
            pltpu.VMEM((4, CH, CH), BF16),
            pltpu.VMEM((6, CH, 256), BF16),
            pltpu.VMEM((6, CH, 256), BF16),
            pltpu.VMEM((16, CH, 256), BF16),
            pltpu.VMEM((16, 32), jnp.int32),
            pltpu.VMEM((18, 8, COLS), F32),
            pltpu.VMEM((8, 128, 1024), BF16),
            pltpu.VMEM((2, HALF, 2048), BF16),
            pltpu.VMEM((PAR, 2048), BF16),
            pltpu.VMEM((256, PAR), BF16),
            pltpu.VMEM((2, 2048, 128), F32),
            pltpu.VMEM((NT, 16, 256), BF16),
            dma((8,)),
            dma((5,)),
            dma((4,)),
            dma((4,)),
            dma((5,)),
            dma((5,)),
            dma((2,)),
            dma((2,)),
            pltpu.SemaphoreType.REGULAR((2,)),
            dma((2,)),
            dma((2,)),
            dma((2,)),
            dma((2,)),
        ],
        compiler_params=pltpu.CompilerParams(
            collective_id=0, has_side_effects=True, vmem_limit_bytes=60 << 20
        ),
        name="convs_and_exchange",
    )(feat, valid, owner, w1raw, w2raw, wmraw)


def place_kernel(recv, enh, out, enh_out, got16, r32, o, hop, mine, sem, rsem, psem):
    parts = [pl.ds(8 * i, 8) for i in range(4)]
    ins = [pltpu.make_async_copy(enh.at[p], hop.at[p], sem.at[i]) for i, p in enumerate(parts)]
    outs = [pltpu.make_async_copy(hop.at[p], enh_out.at[p], sem.at[i]) for i, p in enumerate(parts)]
    some = [
        pltpu.make_async_copy(recv.at[pl.ds(32 * i, 32)], got16.at[pl.ds(32 * i, 32)], rsem.at[i])
        for i in range(4)
    ]
    for copy in some + ins:
        copy.start()

    for first in range(0, NT, 32):
        some[first // 32].wait()

        def widen(i, carry):
            for d2 in range(2):
                part = got16[pl.ds(8 * i, 8), :, pl.ds(d2 * 128, 128)].reshape(128, 128)
                r32[d2, pl.ds(pl.multiple_of(128 * i, 128), 128)] = part.astype(F32)
            return carry

        lax.fori_loop(first // 8, first // 8 + 4, widen, 0)
    here = [jnp.where(r32[0, pl.ds(k, 128, stride=16), :] < EMPTY, 1.0, 0.0) for k in range(2)]
    count = dot_t(ones_at((8, NT), lambda i, j: j == 0), (here[0] + here[1]).astype(BF16))
    start = dot(count.astype(BF16), ones_at((NT, NT), lambda i, j: i < j))
    slot = lax.broadcasted_iota(jnp.int32, (CAP, NT), 0).astype(F32)
    count = jnp.broadcast_to(count[0:1], (CAP, NT))
    start = jnp.broadcast_to(start[0:1], (CAP, NT))
    pick = jnp.concatenate(
        [
            jnp.where((slot == start + float(k)) & (count > float(k)), 1.0, 0.0)
            for k in range(2)
        ],
        axis=1,
    ).astype(BF16)
    by_four = ones_at((256, 256), lambda i, j: j == i % 32 // 4 * 32 + i // 32 * 4 + i % 4)
    for v in range(8):
        got = jnp.concatenate(
            [
                jnp.concatenate(
                    [r32[d2, pl.ds(v * 2 + k, 128, stride=16), :] for d2 in range(2)], axis=1
                )
                for k in range(2)
            ],
            axis=0,
        ).astype(BF16)
        o[v] = dot(dot(pick, got).astype(BF16), by_four).astype(BF16)
    for first, second in zip(ins, outs):
        first.wait()
        second.start()
    turn = ones_at((256, 256), lambda i, j: j == i % 8 * 32 + i // 8 % 8 * 4 + i // 64)
    lane = lax.broadcasted_iota(jnp.int32, (CAP, 128), 1) // 32
    for q in range(8):
        w, pos = q // 4, q % 4
        halves = []
        for hv in range(2):
            acc = jnp.zeros((CAP, 128), BF16)
            for i in range(4):
                part = o[hv * 4 + i, :, pl.ds(w * 128, 128)]
                if i != pos:
                    part = pltpu.roll(part, (32 * (i - pos)) % 128, 1)
                acc = jnp.where(lane == i, part, acc)
            halves.append(acc)
        last = dot_t(turn, jnp.concatenate(halves, axis=1)).astype(BF16)
        for i in range(4):
            mine[q * 4 + i] = last[i * 64 : i * 64 + 64]
        outs.append(
            pltpu.make_async_copy(mine.at[pl.ds(4 * q, 4)], out.at[pl.ds(4 * q, 4)], psem.at[q])
        )
        outs[-1].start()
    for copy in outs:
        copy.wait()


def place_call(recv, enh):
    any_ = pl.BlockSpec(memory_space=pl.ANY)
    return pl.pallas_call(
        place_kernel,
        out_shape=(
            jax.ShapeDtypeStruct((HC, 64, CAP), BF16),
            jax.ShapeDtypeStruct((HC, ROWS, COLS), BF16),
        ),
        in_specs=[any_, any_],
        out_specs=(any_, any_),
        scratch_shapes=[
            pltpu.VMEM((NT, 16, 256), BF16),
            pltpu.VMEM((2, 2048, 128), F32),
            pltpu.VMEM((8, CAP, 256), BF16),
            pltpu.VMEM((HC, ROWS, COLS), BF16),
            pltpu.VMEM((HC, 64, CAP), BF16),
            pltpu.SemaphoreType.DMA((4,)),
            pltpu.SemaphoreType.DMA((4,)),
            pltpu.SemaphoreType.DMA((8,)),
        ],
        compiler_params=pltpu.CompilerParams(vmem_limit_bytes=60 << 20),
        name="place_parents",
    )(recv, enh)


def on_device(features, tile_valid, parent_owner, w_first, w_second, w_merge):
    enh, recv = main_call(
        features, tile_valid, parent_owner.reshape(1, PAR), w_first, w_second,
        jnp.transpose(w_merge, (0, 2, 1)),
    )
    parents, enhanced = place_call(recv, enh)
    return (enhanced, jnp.transpose(parents, (0, 2, 1)))


def solution(mesh):
    return jax.shard_map(
        on_device,
        mesh=mesh,
        in_specs=(
            P("chan", "tiles", None),
            P("tiles", None),
            P("tiles"),
            P(None, "chan", None),
            P(None, "chan", None),
            P(None, None, "chan"),
        ),
        out_specs=(P("chan", "tiles", None), P("chan", "tiles", None)),
        check_vma=False,
    )
```
